32 devices in a mesh: kx: 4 (over y, core), ky: 8 (over z, x).
Axes of the slice: x: 2, y: 2, z: 4, core: 2. Of those that a mesh axis runs over, the one named last changes fastest.
Arguments:
- packed_state_matrix: float32 [16, 128, 1024], P(None, 'kx', 'ky'), may hold values from -1 to 1, as said below
- energies: float32 [4, 128, 1024], P(None, 'kx', 'ky'), may hold values from -2.4 to 2.4
- dipole_x: float32 [12, 128, 1024], P(None, 'kx', 'ky'), may hold values from -2.5 to 2.5
- dipole_y: float32 [12, 128, 1024], P(None, 'kx', 'ky'), may hold values from -2.5 to 2.5
- interaction: float32 [128, 1024], P('ky'), may hold values from 0.3 to 5, as said below
- driving_field: float32 [2], replicated, may hold values from 0.3 to 1
Outputs:
- section_slope: float32 [16, 128, 1024], P(None, 'kx', 'ky')
- field_next: float32 [2], replicated
The draws below stay inside these ranges and needn't reach their ends.
Inputs may be any that keep to these rules, and one draw needn't show every extreme that they name: `packed_state_matrix`: components 0 to 3 lie in 0 to 1. interaction at (p, q) equals interaction at ((-p) mod 128, q) and at (p, (-q) mod 1024).
All inputs are finite; a program needn't handle non-finite values.
Results may differ from the reference program's by a relative error of at most 0.000054.
Values sent between devices are 32-bit elements; how exact they have to be, the bound alone decides.
A program may use at most 64 MiB of HBM per device.

```python
import jax
import jax.numpy as jnp
from jax import lax

NKX = 128
NKY = 1024


def band_fields(key):
    disorder_seed = jax.random.fold_in(key, 101)
    row_key = jax.random.fold_in(key, 102)
    column_key = jax.random.fold_in(key, 103)
    row_place = jnp.arange(NKX, dtype=jnp.float32) / NKX
    column_place = jnp.arange(NKY, dtype=jnp.float32) / NKY
    roughness = jnp.clip(0.4 * jax.random.normal(disorder_seed, (4, NKX, NKY), jnp.float32), -0.8, 0.8)
    row_exponent = 0.5 * row_place + 0.5 * jax.random.uniform(row_key, (NKX,), jnp.float32)
    second_power_order = 0.5 * column_place + 0.5 * jax.random.uniform(column_key, (NKY,), jnp.float32)
    offsets = jnp.array([-1.6, -1.0, 1.0, 1.6], jnp.float32)
    energies = offsets[:, None, None] + roughness
    shifted = 0.5 * (jnp.roll(energies, 1, axis=1) + jnp.roll(energies, 1, axis=2))
    occupied = jax.nn.sigmoid(-2.0 * shifted)
    weight_grid = jnp.power(10.0, row_exponent[:, None] + second_power_order[None, :] - 2.0)
    return (energies, occupied * weight_grid[None])


def draw_packed_state_matrix(key, part):
    energies, populations = band_fields(key)
    coherence_key = jax.random.fold_in(key, 104)
    coherences = jnp.clip(0.25 * jax.random.normal(coherence_key, (12, NKX, NKY), jnp.float32), -1.0, 1.0)
    return jnp.concatenate([populations, coherences])


def draw_energies(key, part):
    energies, populations = band_fields(key)
    return energies


def mirror(values, axis_direction):
    return jnp.roll(jnp.flip(values, axis_direction), 1, axis_direction)


def draw_interaction(key, part):
    raw_key = jax.random.fold_in(key, 105)
    unscaled_values = jax.random.uniform(raw_key, (NKX, NKY), jnp.float32, 0.4, 4.0)
    return 0.25 * (unscaled_values + mirror(unscaled_values, 0) + mirror(unscaled_values, 1) + mirror(mirror(unscaled_values, 0), 1))


def steps_of(stream_key, dims, split, smallest, high):
    level, own = 1.0, jax.random.fold_in(stream_key, 6)
    for axis_at, parts in split:
        steps = jnp.exp(jax.random.uniform(jax.random.fold_in(own, axis_at), (parts,), jnp.float32, smallest / len(split), high / len(split)))
        level = level * jnp.repeat(steps, dims[axis_at] // parts).reshape([-1 if axis == axis_at else 1 for axis in range(len(dims))])
    return level


def centred(stream_key, dims, deviation, most, split=(), kind=jnp.bfloat16):
    values = deviation * jax.random.normal(stream_key, dims, jnp.float32)
    if split:
        values = values * steps_of(stream_key, dims, split, -0.22, 0.18)
    return jnp.clip(values, -most, most).astype(kind)


def setup_inputs(seed: int = 0) -> dict:
    keys = jax.random.split(jax.random.key(seed), 7)
    packed_state_matrix = draw_packed_state_matrix(jax.random.fold_in(keys[6], 71), 0)
    energies = draw_energies(jax.random.fold_in(keys[6], 71), 0)
    dipole_x = centred(keys[2], (12, NKX, NKY), 0.3, 2.5, ((1, 4), (2, 8)), jnp.float32)
    dipole_y = centred(keys[3], (12, NKX, NKY), 0.3, 2.5, ((1, 4), (2, 8)), jnp.float32)
    interaction = draw_interaction(jax.random.fold_in(keys[6], 71), 0)
    driving_field = jnp.clip(jax.random.uniform(keys[5], (2,), jnp.float32, 0.3, 1.0), 0.3, 1.0)
    return {"packed_state_matrix": packed_state_matrix, "energies": energies, "dipole_x": dipole_x, "dipole_y": dipole_y, "interaction": interaction, "driving_field": driving_field}


BAND_PAIRS = ((0, 1), (0, 2), (0, 3), (1, 2), (1, 3), (2, 3))
DEPHASING = 0.5
SHIELDING_LEVEL = 2.0
COUPLING = 40.0


def unpack(packed):
    real_entries = []
    imaginary_entries = []
    for band_one in range(4):
        real_entries.append([None, None, None, None])
        imaginary_entries.append([None, None, None, None])
    for band_one in range(4):
        real_entries[band_one][band_one] = packed[band_one]
    for number, band_pair in enumerate(BAND_PAIRS):
        upper_band, lower_band = band_pair
        real_entries[upper_band][lower_band] = packed[4 + number]
        real_entries[lower_band][upper_band] = packed[4 + number]
        imaginary_entries[upper_band][lower_band] = packed[10 + number]
        imaginary_entries[lower_band][upper_band] = -packed[10 + number]
    return real_entries, imaginary_entries


def product_sum(terms):
    summed = None
    for factor, left_value, right_value in terms:
        if left_value is None or right_value is None:
            continue
        product = factor * left_value * right_value
        summed = product if summed is None else summed + product
    return summed


def commutator(coupled, packed_state_matrix):
    coupled_real, coupled_imaginary = unpack(coupled)
    state_real, state_imaginary = unpack(packed_state_matrix)

    def element(row_band, column_band):
        real_terms = []
        imaginary_terms = []
        for middle in range(4):
            real_terms.append((1.0, coupled_real[row_band][middle], state_real[middle][column_band]))
            real_terms.append((-1.0, coupled_imaginary[row_band][middle], state_imaginary[middle][column_band]))
            real_terms.append((-1.0, state_real[row_band][middle], coupled_real[middle][column_band]))
            real_terms.append((1.0, state_imaginary[row_band][middle], coupled_imaginary[middle][column_band]))
            imaginary_terms.append((1.0, coupled_real[row_band][middle], state_imaginary[middle][column_band]))
            imaginary_terms.append((1.0, coupled_imaginary[row_band][middle], state_real[middle][column_band]))
            imaginary_terms.append((-1.0, state_real[row_band][middle], coupled_imaginary[middle][column_band]))
            imaginary_terms.append((-1.0, state_imaginary[row_band][middle], coupled_real[middle][column_band]))
        return product_sum(real_terms), product_sum(imaginary_terms)

    diagonal = []
    upper_real = []
    upper_imaginary = []
    for band_one in range(4):
        diagonal.append(element(band_one, band_one)[1])
    for upper_band, lower_band in BAND_PAIRS:
        real_value, imaginary_value = element(upper_band, lower_band)
        upper_real.append(imaginary_value)
        upper_imaginary.append(-real_value)
    return jnp.stack(diagonal + upper_real + upper_imaginary)


def slope_terms(packed_state_matrix, energies, self_energy, gradient_x, gradient_y, dipole_x, dipole_y, driving_field):
    field_x = driving_field[0]
    field_y = driving_field[1]
    coupled = jnp.concatenate([energies + self_energy[0:4], self_energy[4:16] + field_x * dipole_x + field_y * dipole_y])
    rotation = commutator(coupled, packed_state_matrix)
    drift = rotation + field_x * gradient_x + field_y * gradient_y
    return jnp.concatenate([drift[0:4], drift[4:16] - DEPHASING * packed_state_matrix[4:16]])


def grid_derivative(values, axis_direction):
    step_ahead = jnp.roll(values, -1, axis_direction)
    step_behind = jnp.roll(values, 1, axis_direction)
    two_ahead = jnp.roll(values, -2, axis_direction)
    two_behind = jnp.roll(values, 2, axis_direction)
    return (8.0 * (step_ahead - step_behind) - (two_ahead - two_behind)) / 12.0


def reference(packed_state_matrix, energies, dipole_x, dipole_y, interaction, driving_field):
    primitive_tile_total = NKX * NKY
    gradient_x = grid_derivative(packed_state_matrix, 1)
    gradient_y = grid_derivative(packed_state_matrix, 2)
    velocity_x = grid_derivative(energies, 1)
    group_velocity_y = grid_derivative(energies, 2)
    electron_population = jnp.sum(packed_state_matrix[2] + packed_state_matrix[3]) / primitive_tile_total
    current_x = jnp.sum(velocity_x * packed_state_matrix[0:4]) / primitive_tile_total
    current_y = jnp.sum(group_velocity_y * packed_state_matrix[0:4]) / primitive_tile_total
    shielding_multiplier = 1.0 / (1.0 + SHIELDING_LEVEL * electron_population)

    def convolve_one(component):
        spectrum = jnp.fft.fft2(component) * interaction
        return jnp.real(jnp.fft.ifft2(spectrum)).astype(jnp.float32)

    convolved = lax.map(convolve_one, packed_state_matrix)
    self_energy = -shielding_multiplier * convolved
    section_slope = slope_terms(packed_state_matrix, energies, self_energy, gradient_x, gradient_y, dipole_x, dipole_y, driving_field)
    field_next = driving_field - COUPLING * jnp.stack([current_x, current_y])
    return section_slope, field_next
```

```python
from functools import partial
import math

import jax
import jax.numpy as jnp
import ml_dtypes
import numpy as np
from jax import lax
from jax.experimental import pallas as pl
from jax.experimental.pallas import tpu as pltpu
from jax.sharding import PartitionSpec as P

BAND_PAIRS = ((0, 1), (0, 2), (0, 3), (1, 2), (1, 3), (2, 3))
DEPHASING = 0.5
SHIELDING_LEVEL = 2.0
COUPLING = 40.0


def with_halo(array, sides, width):
    for axis, dim in sides:
        devices, length = (lax.axis_size(axis), array.shape[dim])
        up = [(i, (i + 1) % devices) for i in range(devices)]
        down = [(j, i) for i, j in up]
        last = lax.slice_in_dim(array, length - width, length, axis=dim)
        initial = lax.slice_in_dim(array, 0, width, axis=dim)
        before = lax.ppermute(last, axis, up)
        after = lax.ppermute(initial, axis, down)
        array = jnp.concatenate([before, array, after], axis=dim)
    return array


def unpack(packed):
    real_entries = []
    imaginary_entries = []
    for band_one in range(4):
        real_entries.append([None, None, None, None])
        imaginary_entries.append([None, None, None, None])
    for band_one in range(4):
        real_entries[band_one][band_one] = packed[band_one]
    for number, band_pair in enumerate(BAND_PAIRS):
        upper_band, lower_band = band_pair
        real_entries[upper_band][lower_band] = packed[4 + number]
        real_entries[lower_band][upper_band] = packed[4 + number]
        imaginary_entries[upper_band][lower_band] = packed[10 + number]
        imaginary_entries[lower_band][upper_band] = -packed[10 + number]
    return (real_entries, imaginary_entries)


def product_sum(terms):
    summed = None
    for factor, left_value, right_value in terms:
        if left_value is None or right_value is None:
            continue
        product = factor * left_value * right_value
        summed = product if summed is None else summed + product
    return summed


def commutator(coupled, packed_state_matrix):
    coupled_real, coupled_imaginary = unpack(coupled)
    state_real, state_imaginary = unpack(packed_state_matrix)

    def element(row_band, column_band):
        real_terms = []
        imaginary_terms = []
        for middle in range(4):
            real_terms.append(
                (1.0, coupled_real[row_band][middle], state_real[middle][column_band])
            )
            real_terms.append(
                (-1.0, coupled_imaginary[row_band][middle], state_imaginary[middle][column_band])
            )
            real_terms.append(
                (-1.0, state_real[row_band][middle], coupled_real[middle][column_band])
            )
            real_terms.append(
                (1.0, state_imaginary[row_band][middle], coupled_imaginary[middle][column_band])
            )
            imaginary_terms.append(
                (1.0, coupled_real[row_band][middle], state_imaginary[middle][column_band])
            )
            imaginary_terms.append(
                (1.0, coupled_imaginary[row_band][middle], state_real[middle][column_band])
            )
            imaginary_terms.append(
                (-1.0, state_real[row_band][middle], coupled_imaginary[middle][column_band])
            )
            imaginary_terms.append(
                (-1.0, state_imaginary[row_band][middle], coupled_real[middle][column_band])
            )
        return (product_sum(real_terms), product_sum(imaginary_terms))

    diagonal = []
    upper_real = []
    upper_imaginary = []
    for band_one in range(4):
        diagonal.append(element(band_one, band_one)[1])
    for upper_band, lower_band in BAND_PAIRS:
        real_value, imaginary_value = element(upper_band, lower_band)
        upper_real.append(imaginary_value)
        upper_imaginary.append(-real_value)
    return jnp.stack(diagonal + upper_real + upper_imaginary)


def slope_terms(
    packed_state_matrix,
    energies,
    self_energy,
    gradient_x,
    gradient_y,
    dipole_x,
    dipole_y,
    driving_field,
):
    field_x = driving_field[0]
    field_y = driving_field[1]
    coupled = jnp.concatenate(
        [energies + self_energy[0:4], self_energy[4:16] + field_x * dipole_x + field_y * dipole_y]
    )
    rotation = commutator(coupled, packed_state_matrix)
    drift = rotation + field_x * gradient_x + field_y * gradient_y
    return jnp.concatenate([drift[0:4], drift[4:16] - DEPHASING * packed_state_matrix[4:16]])


def angle_table(row_count, column_count, period, direction):
    row_index = lax.broadcasted_iota(jnp.int32, (row_count, column_count), 0)
    column_index = lax.broadcasted_iota(jnp.int32, (row_count, column_count), 1)
    phase_angle = (row_index * column_index % period).astype(jnp.float32) * (
        direction * 2.0 * math.pi / period
    )
    return (jnp.cos(phase_angle), jnp.sin(phase_angle))


def complex_contract(einsum_form, data_real, data_imaginary, table_real, table_imaginary):
    contract = partial(
        jnp.einsum, precision=lax.Precision.HIGHEST, preferred_element_type=jnp.float32
    )
    if data_imaginary is None:
        return (
            contract(einsum_form, data_real, table_real),
            contract(einsum_form, data_real, table_imaginary),
        )
    real_out = contract(einsum_form, data_real, table_real) - contract(
        einsum_form, data_imaginary, table_imaginary
    )
    imaginary_out = contract(einsum_form, data_real, table_imaginary) + contract(
        einsum_form, data_imaginary, table_real
    )
    return (real_out, imaginary_out)


def transform(data_real, data_imaginary, direction, along_last):
    length = data_real.shape[-1] if along_last else data_real.shape[-2]
    outer_size = 16
    inner_size = length // outer_size
    outer_cosine, outer_sine = angle_table(outer_size, outer_size, outer_size, direction)
    twist_cosine, twist_sine = angle_table(outer_size, inner_size, length, direction)
    inner_cosine, inner_sine = angle_table(inner_size, inner_size, inner_size, direction)
    if along_last:
        split_shape = data_real.shape[:-1] + (outer_size, inner_size)
        first_form = "...aq,ab->...bq"
        second_form = "...bq,qc->...cb"
    else:
        split_shape = data_real.shape[:-2] + (outer_size, inner_size, data_real.shape[-1])
        first_form = "...aqt,ab->...bqt"
        second_form = "...bqt,qc->...cbt"
        twist_cosine = twist_cosine[:, :, None]
        twist_sine = twist_sine[:, :, None]
    part_real = data_real.reshape(split_shape)
    part_imaginary = None if data_imaginary is None else data_imaginary.reshape(split_shape)
    section_real, section_imaginary = complex_contract(
        first_form, part_real, part_imaginary, outer_cosine, outer_sine
    )
    turned_real = section_real * twist_cosine - section_imaginary * twist_sine
    turned_imaginary = section_real * twist_sine + section_imaginary * twist_cosine
    final_real, final_imaginary = complex_contract(
        second_form, turned_real, turned_imaginary, inner_cosine, inner_sine
    )
    return (final_real.reshape(data_real.shape), final_imaginary.reshape(data_real.shape))


def convolve(source, interaction, primitive_tile_total):
    along_kx = lax.all_to_all(source, "kx", split_axis=0, concat_axis=1, tiled=True)
    broad_nonimaginary, wide_imaginary = transform(along_kx, None, -1.0, False)
    joined = jnp.stack([broad_nonimaginary, wide_imaginary])
    along_ky = lax.all_to_all(joined, "ky", split_axis=2, concat_axis=3, tiled=True)
    line_real, line_imaginary = transform(along_ky[0], along_ky[1], -1.0, True)
    line_real, line_imaginary = transform(
        line_real * interaction, line_imaginary * interaction, 1.0, True
    )
    returned = lax.all_to_all(
        jnp.stack([line_real, line_imaginary]), "ky", split_axis=3, concat_axis=2, tiled=True
    )
    final_real, final_imaginary = transform(returned[0], returned[1], 1.0, False)
    normalizer = 1.0 / primitive_tile_total
    return lax.all_to_all(final_real * normalizer, "kx", split_axis=1, concat_axis=0, tiled=True)


def collect_moments(local_sums, primitive_tile_total):
    return lax.psum(local_sums, ("kx", "ky")) / primitive_tile_total


def body(packed_state_matrix, energies, dipole_x, dipole_y, interaction, driving_field):
    rows_local = packed_state_matrix.shape[1]
    columns_local = packed_state_matrix.shape[2]
    primitive_tile_total = rows_local * columns_local * lax.axis_size("kx") * lax.axis_size("ky")
    stacked = jnp.concatenate([packed_state_matrix, energies])
    padded = with_halo(stacked, (("kx", 1), ("ky", 2)), 2)
    column_core = padded[:, :, 2:-2]
    row_core = padded[:, 2:-2, :]
    gradient_x = (
        8.0 * (column_core[:, 3:-1] - column_core[:, 1:-3])
        - (column_core[:, 4:] - column_core[:, :-4])
    ) / 12.0
    gradient_y = (
        8.0 * (row_core[:, :, 3:-1] - row_core[:, :, 1:-3])
        - (row_core[:, :, 4:] - row_core[:, :, :-4])
    ) / 12.0
    populations = packed_state_matrix[0:4]
    local_sums = jnp.stack(
        [
            jnp.sum(packed_state_matrix[2] + packed_state_matrix[3]),
            jnp.sum(gradient_x[16:20] * populations),
            jnp.sum(gradient_y[16:20] * populations),
        ]
    )
    totals = collect_moments(local_sums, primitive_tile_total)
    shielding_multiplier = 1.0 / (1.0 + SHIELDING_LEVEL * totals[0])
    self_energy = -convolve(
        packed_state_matrix * shielding_multiplier, interaction, primitive_tile_total
    )
    section_slope = slope_terms(
        packed_state_matrix,
        energies,
        self_energy,
        gradient_x[0:16],
        gradient_y[0:16],
        dipole_x,
        dipole_y,
        driving_field,
    )
    field_next = driving_field - COUPLING * totals[1:3]
    return (section_slope, field_next)


def split_table(values):
    high = values.astype(ml_dtypes.bfloat16)
    low = (values - high.astype(np.float64)).astype(ml_dtypes.bfloat16)
    return high, low


def kx_table(upper):
    length = 128
    x = np.arange(length)
    rows = []
    for half in range(2):
        positions = np.arange(32 * half, 32 * half + 32)
        if upper:
            orders = 16 * (positions // 16) + 16 - positions % 16
        else:
            orders = positions
        cosine = np.cos(2 * np.pi * (np.outer(orders, x) % length) / length)
        sine = np.sin(2 * np.pi * (np.outer(orders, x) % length) / length)
        cosine *= np.where((orders == 0) | (orders == 64), 1.0, np.sqrt(2.0))[:, None]
        sine *= np.sqrt(2.0)
        for at, order in enumerate(orders):
            if not upper and order == 0:
                sine[at] = np.where(x % 2 == 0, 1.0, -1.0)
            if upper and order == 64:
                sine[at] = 1.0
        rows += [cosine, sine]
    return np.concatenate(rows) / np.sqrt(length)


def ky_tables():
    length = 1024
    k = np.arange(512)[:, None]

    def waves(orders, reach):
        angle = 2 * np.pi * (k[:reach] * orders[None, :] % length) / length
        return np.cos(angle), np.sin(angle)

    m = np.arange(128)
    scale = np.sqrt(2.0 / length)
    cosine, sine = waves(4 * m, 256)
    cosine, sine = cosine * scale, sine * scale
    cosine[:, 0] = np.sqrt(1.0 / length)
    sine[:, 0] = np.where(np.arange(256) % 2 == 0, 1.0, -1.0) * np.sqrt(1.0 / length)
    first = np.concatenate([cosine, sine], axis=1)
    cosine, sine = waves(4 * m + 2, 256)
    second = np.concatenate([cosine, sine], axis=1) * scale
    cosine, sine = waves(4 * np.arange(256) + 1, 512)
    third = np.concatenate([cosine, sine], axis=1) * scale
    return first, second, third


def pick_table():
    m = np.arange(128)
    wanted = np.concatenate([4 * m, 4 * m + 2, 4 * np.arange(256) + 1, np.full(128, 512)])
    table = np.zeros((1024, 640))
    table[wanted, np.arange(640)] = 1.0
    return table


MESH = pl.DeviceIdType.MESH
COMPONENTS = 16
ROWS, COLUMNS = 32, 128
KX_DEVICES, KY_DEVICES = 4, 8


def fits_section_kernel(mesh):
    return (mesh.shape["kx"], mesh.shape["ky"]) == (KX_DEVICES, KY_DEVICES)


def bf16_parts(values):
    high = values.astype(jnp.bfloat16)
    low = (values - high.astype(jnp.float32)).astype(jnp.bfloat16)
    return high, low


def matmul(left, right):
    return jnp.dot(left, right, preferred_element_type=jnp.float32)


def rows_by_table(values, table_high, table_low):
    count = values.shape[0]
    high, low = bf16_parts(values)
    both = matmul(jnp.concatenate([high, low], axis=0), table_high)
    return both[:count] + both[count:] + matmul(high, table_low)


def table_by_columns(table, values):
    high, low = bf16_parts(values)
    return matmul(table, jnp.concatenate([high, low, high], axis=0))


def section_kernel(
    rho, energies, dipole_x, dipole_y, interaction, field,
    kx_forward, kx_back, ky_short, ky_long, pick,
    out, field_out,
    lines, conv, halo_out, halo_in, columns_out, columns_in, extended,
    weights_own, weights, weight_special, turned, turned_in, back, final,
    sums_kx, sums_ky, static_part,
    short_table, long_table, pick_table_vmem,
    table_sem, send_sem, line_sem, halo_send, halo_recv, weight_send, weight_recv,
    pair_send, pair_recv, return_send, return_recv, sum_send, sum_recv,
):
    i = lax.axis_index("kx")
    j = lax.axis_index("ky")
    chip_y = i // 2
    half = i % 2
    upper = j // 4
    component = chip_y * 8 + j

    tables = [
        pltpu.make_async_copy(pick, pick_table_vmem, table_sem.at[0]),
        pltpu.make_async_copy(ky_short, short_table, table_sem.at[1]),
        pltpu.make_async_copy(ky_long, long_table, table_sem.at[2]),
    ]
    for table in tables:
        table.start()

    barrier = pltpu.get_barrier_semaphore()

    def greet(device, carry):
        @pl.when(device != i * KY_DEVICES + j)
        def _():
            pl.semaphore_signal(
                barrier, inc=1, device_id=(device // KY_DEVICES, device % KY_DEVICES), device_id_type=MESH
            )

        return carry

    lax.fori_loop(0, KX_DEVICES * KY_DEVICES, greet, 0)

    def remote(source, target, send, receive, device):
        return pltpu.make_async_remote_copy(
            src_ref=source, dst_ref=target, send_sem=send, recv_sem=receive,
            device_id=device, device_id_type=MESH,
        )

    def await_bytes(ref, semaphore):
        pltpu.make_async_copy(ref, ref, semaphore).wait()

    lane = lax.broadcasted_iota(jnp.int32, (ROWS, COLUMNS), 1)
    packed_columns = jnp.zeros((ROWS, COLUMNS), jnp.float32)
    for c in range(COMPONENTS):
        plane = rho[c]
        halo_out[0, 2 * c : 2 * c + 2, :] = plane[0:2]
        halo_out[1, 2 * c : 2 * c + 2, :] = plane[ROWS - 2 : ROWS]
        first = pltpu.roll(plane, 2 * c, 1) if c else plane
        last = pltpu.roll(plane, 66 + 2 * c, 1)
        packed_columns = jnp.where((lane // 2) == c, first, packed_columns)
        packed_columns = jnp.where((lane // 2) == 32 + c, last, packed_columns)
        extended[c, 8 : 8 + ROWS, :] = plane
    columns_out[...] = packed_columns

    pl.semaphore_wait(barrier, KX_DEVICES * KY_DEVICES - 1)

    def forward_target(step):
        c = (component + 1 + step) % COMPONENTS
        return c, 2 * (c // 8) + upper, c % 8

    def send_forward(step, carry):
        c, target_i, target_j = forward_target(step)
        slot = i * 4 + j % 4
        target = lines.at[j % 4, pl.ds(pl.multiple_of(ROWS * i, ROWS), ROWS), :]
        own = (target_i == i) & (target_j == j)

        @pl.when(jnp.logical_not(own))
        def _():
            remote(rho.at[c], target, send_sem.at[step], line_sem.at[slot], (target_i, target_j)).start()

        @pl.when(own)
        def _():
            pltpu.make_async_copy(rho.at[c], target, line_sem.at[slot]).start()

        return carry

    lax.fori_loop(0, COMPONENTS, send_forward, 0)

    before_i, after_i = (i + KX_DEVICES - 1) % KX_DEVICES, (i + 1) % KX_DEVICES
    before_j, after_j = (j + KY_DEVICES - 1) % KY_DEVICES, (j + 1) % KY_DEVICES
    halo_copies = [
        remote(halo_out.at[0], halo_in.at[1], halo_send.at[0], halo_recv.at[0], (before_i, j)),
        remote(halo_out.at[1], halo_in.at[0], halo_send.at[1], halo_recv.at[1], (after_i, j)),
        remote(columns_out, columns_in.at[1], halo_send.at[2], halo_recv.at[2], (i, before_j)),
        remote(columns_out, columns_in.at[0], halo_send.at[3], halo_recv.at[3], (i, after_j)),
    ]
    for copy in halo_copies:
        copy.start()

    tables[0].wait()
    high = interaction[...].astype(jnp.bfloat16)
    rest = interaction[...] - high.astype(jnp.float32)
    middle = rest.astype(jnp.bfloat16)
    low = (rest - middle.astype(jnp.float32)).astype(jnp.bfloat16)
    picked = matmul(jnp.concatenate([high, middle, low], axis=0), pick_table_vmem[...])
    weights_own[...] = picked[0:16] + picked[16:32] + picked[32:48]

    block = jnp.where(upper == 0, j, 7 - j)
    sends_weights = half == block // 2
    sends_special = ((j == 4) & (half == 0)) | ((j == 0) & (half == 1))
    special_group = 1 - upper

    def send_weights(step, carry):
        target_j = 4 * upper + step
        target = weights.at[pl.ds(pl.multiple_of(16 * (block % 2), 16), 16), :]

        @pl.when(sends_weights & (target_j != j))
        def _():
            remote(
                weights_own, target, weight_send.at[step], weight_recv.at[block % 2], (i, target_j)
            ).start()

        @pl.when(sends_weights & (target_j == j))
        def _():
            pltpu.make_async_copy(weights_own, target, weight_recv.at[block % 2]).start()

        @pl.when(sends_special)
        def _():
            remote(
                weights_own.at[pl.ds(0, 8), :], weight_special, weight_send.at[step], weight_recv.at[2],
                (i, 4 * special_group + step),
            ).start()

        return carry

    lax.fori_loop(0, 4, send_weights, 0)

    for copy in halo_copies:
        copy.wait_recv()
    field_x = field[0]
    field_y = field[1]
    left_columns = columns_in[0]
    right_columns = columns_in[1]
    carriers_part = jnp.zeros((ROWS, COLUMNS), jnp.float32)
    current_x_part = jnp.zeros((ROWS, COLUMNS), jnp.float32)
    current_y_part = jnp.zeros((ROWS, COLUMNS), jnp.float32)
    for c in range(COMPONENTS):
        extended[c, 6:8, :] = halo_in[0, 2 * c : 2 * c + 2, :]
        extended[c, 8 + ROWS : 10 + ROWS, :] = halo_in[1, 2 * c : 2 * c + 2, :]
        plane = rho[c]
        gradient_x = (
            8.0 * (extended[c, 9 : 9 + ROWS, :] - extended[c, 7 : 7 + ROWS, :])
            - (extended[c, 10 : 10 + ROWS, :] - extended[c, 6 : 6 + ROWS, :])
        ) * (1.0 / 12.0)
        ahead_edge = pltpu.roll(right_columns, (127 - 2 * c) % 128, 1)
        ahead_two_edge = pltpu.roll(right_columns, (126 - 2 * c) % 128, 1)
        behind_edge = pltpu.roll(left_columns, (63 - 2 * c) % 128, 1)
        behind_two_edge = pltpu.roll(left_columns, 64 - 2 * c, 1)
        ahead = jnp.where(lane >= 127, ahead_edge, pltpu.roll(plane, 127, 1))
        ahead_two = jnp.where(lane >= 126, ahead_two_edge, pltpu.roll(plane, 126, 1))
        behind = jnp.where(lane < 1, behind_edge, pltpu.roll(plane, 1, 1))
        behind_two = jnp.where(lane < 2, behind_two_edge, pltpu.roll(plane, 2, 1))
        gradient_y = (8.0 * (ahead - behind) - (ahead_two - behind_two)) * (1.0 / 12.0)
        drift = field_x * gradient_x + field_y * gradient_y
        if c < 4:
            current_x_part = current_x_part - energies[c] * gradient_x
            current_y_part = current_y_part - energies[c] * gradient_y
            static_part[c] = energies[c]
        else:
            drift = drift - DEPHASING * plane
            static_part[c] = field_x * dipole_x[c - 4] + field_y * dipole_y[c - 4]
        if c in (2, 3):
            carriers_part = carriers_part + plane
        out[c] = drift

    def lane_sums(part):
        folded = part[0:8] + part[8:16] + part[16:24] + part[24:32]
        return jnp.sum(folded, axis=0, keepdims=True)

    sums_kx[i] = jnp.concatenate(
        [
            lane_sums(carriers_part), lane_sums(current_x_part), lane_sums(current_y_part),
            jnp.zeros((5, COLUMNS), jnp.float32),
        ],
        axis=0,
    )

    def send_sums_kx(step, carry):
        target = (i + 1 + step) % KX_DEVICES
        remote(sums_kx.at[i], sums_kx.at[i], sum_send.at[step], sum_recv.at[i], (target, j)).start()
        return carry

    lax.fori_loop(0, KX_DEVICES - 1, send_sums_kx, 0)

    def await_line(slot, carry):
        await_bytes(
            lines.at[slot % 4, pl.ds(pl.multiple_of(ROWS * (slot // 4), ROWS), ROWS), :], line_sem.at[slot]
        )
        return carry

    lax.fori_loop(0, COMPONENTS, await_line, 0)
    whole_lines = jnp.concatenate([lines[0], lines[1], lines[2], lines[3]], axis=1)
    turned[...] = table_by_columns(kx_forward[upper], whole_lines)

    own_rows = pl.ds(pl.multiple_of(64 * half, 64), 64)
    other_rows = pl.ds(pl.multiple_of(64 * (1 - half), 64), 64)
    partner = (2 * chip_y + 1 - half, j)
    outward = remote(turned.at[other_rows, :], turned_in, pair_send.at[0], pair_recv.at[0], partner)
    outward.start()

    def await_sums_kx(step, carry):
        source = (i + 1 + step) % KX_DEVICES
        await_bytes(sums_kx.at[source], sum_recv.at[source])
        return carry

    lax.fori_loop(0, KX_DEVICES - 1, await_sums_kx, 0)
    sums_ky[j] = (sums_kx[0] + sums_kx[1]) + (sums_kx[2] + sums_kx[3])

    def send_sums_ky(step, carry):
        target = (j + 1 + step) % KY_DEVICES
        remote(
            sums_ky.at[j], sums_ky.at[j], sum_send.at[3 + step], sum_recv.at[KX_DEVICES + j], (i, target)
        ).start()
        return carry

    lax.fori_loop(0, KY_DEVICES - 1, send_sums_ky, 0)

    await_bytes(weights.at[pl.ds(0, 16), :], weight_recv.at[0])
    await_bytes(weights.at[pl.ds(16, 16), :], weight_recv.at[1])

    @pl.when(half == upper)
    def _():
        await_bytes(weight_special, weight_recv.at[2])

    @pl.when(half != upper)
    def _():
        weight_special[...] = jnp.zeros_like(weight_special)

    tables[1].wait()
    tables[2].wait()
    weight_rows = weights[...]
    special = jnp.concatenate([weight_special[0:1, :]] * 32, axis=0)
    row_at = lax.broadcasted_iota(jnp.int32, (32, 640), 0)
    at_special = (row_at == 16 * upper) & (half == upper)
    weight_rows = jnp.concatenate([weight_rows, jnp.where(at_special, special, weight_rows)], axis=0)
    lane_at = lax.broadcasted_iota(jnp.int32, (64, 128), 1)
    weight_sine = jnp.where(lane_at == 0, weight_rows[:, 512:640], weight_rows[:, 0:128])
    weight_first = jnp.concatenate([weight_rows[:, 0:128], weight_sine], axis=1)
    weight_second = jnp.concatenate([weight_rows[:, 128:256]] * 2, axis=1)
    weight_third = jnp.concatenate([weight_rows[:, 256:512]] * 2, axis=1)

    outward.wait_recv()
    sign = jnp.where(half == 0, 1.0, -1.0)
    own = turned[own_rows, :]
    other = turned_in[...]
    even = own + other
    odd = sign * (own - other)
    first = rows_by_table(even[:, :256] + even[:, 256:], short_table[0, 0, :256], short_table[0, 1, :256])
    second = rows_by_table(even[:, :256] - even[:, 256:], short_table[0, 0, 256:], short_table[0, 1, 256:])
    third = rows_by_table(odd, long_table[0, 0], long_table[0, 1])
    first = rows_by_table(first * weight_first, short_table[1, 0, :256], short_table[1, 1, :256])
    second = rows_by_table(second * weight_second, short_table[1, 0, 256:], short_table[1, 1, 256:])
    odd = sign * rows_by_table(third * weight_third, long_table[1, 0], long_table[1, 1])
    even = jnp.concatenate([first + second, first - second], axis=1)
    outward.wait_send()
    turned[own_rows, :] = even - odd
    back[own_rows, :] = even + odd
    homeward = remote(turned.at[own_rows, :], back.at[own_rows, :], pair_send.at[1], pair_recv.at[1], partner)
    homeward.start()

    def await_sums_ky(step, carry):
        source = (j + 1 + step) % KY_DEVICES
        await_bytes(sums_ky.at[source], sum_recv.at[KX_DEVICES + source])
        return carry

    lax.fori_loop(0, KY_DEVICES - 1, await_sums_ky, 0)
    totals = sums_ky[0]
    for source in range(1, KY_DEVICES):
        totals = totals + sums_ky[source]
    point_total = ROWS * COLUMNS * KX_DEVICES * KY_DEVICES
    means = jnp.sum(totals, axis=1, keepdims=True) * (1.0 / point_total)
    screen = 1.0 / (1.0 + SHIELDING_LEVEL * means[0:1, :])
    field_out[0] = field_x - COUPLING * jnp.sum(means[1:2, :])
    field_out[1] = field_y - COUPLING * jnp.sum(means[2:3, :])

    await_bytes(back.at[other_rows, :], pair_recv.at[1])
    convolved = table_by_columns(kx_back[upper], back[...])
    for quarter in range(4):
        final[quarter] = convolved[:, 128 * quarter : 128 * quarter + 128]

    def send_back(step, carry):
        slot = (4 * i + j % 4 + 1 + step) % 16
        target_i = slot // 4
        target_j = 4 * half + slot % 4
        source = final.at[slot % 4, pl.ds(pl.multiple_of(ROWS * target_i, ROWS), ROWS), :]
        own_target = (target_i == i) & (target_j == j)

        @pl.when(jnp.logical_not(own_target))
        def _():
            remote(
                source, conv.at[component], return_send.at[step], return_recv.at[component],
                (target_i, target_j),
            ).start()

        @pl.when(own_target)
        def _():
            pltpu.make_async_copy(source, conv.at[component], return_recv.at[component]).start()

        return carry

    lax.fori_loop(0, COMPONENTS, send_back, 0)

    def await_back(c, carry):
        await_bytes(conv.at[c], return_recv.at[c])
        return carry

    lax.fori_loop(0, COMPONENTS, await_back, 0)

    def rotate(group, carry):
        rows = pl.ds(pl.multiple_of(8 * group, 8), 8)
        coupled = [static_part[c, rows, :] - screen * conv[c, rows, :] for c in range(COMPONENTS)]
        state = [rho[c, rows, :] for c in range(COMPONENTS)]
        rotation = commutator_planes(coupled, state)
        for c in range(COMPONENTS):
            out[c, rows, :] = out[c, rows, :] + rotation[c]
        return carry

    lax.fori_loop(0, ROWS // 8, rotate, 0)

    def drain(step, carry):
        c, target_i, target_j = forward_target(step)

        @pl.when(jnp.logical_not((target_i == i) & (target_j == j)))
        def _():
            await_bytes(rho.at[c], send_sem.at[step])

        slot = (4 * i + j % 4 + 1 + step) % 16

        @pl.when(jnp.logical_not((slot // 4 == i) & (4 * half + slot % 4 == j)))
        def _():
            await_bytes(conv.at[component], return_send.at[step])

        return carry

    lax.fori_loop(0, COMPONENTS, drain, 0)

    def drain_weights(step, carry):
        @pl.when(sends_weights & (4 * upper + step != j))
        def _():
            await_bytes(weights_own, weight_send.at[step])

        @pl.when(sends_special)
        def _():
            await_bytes(weight_special, weight_send.at[step])

        return carry

    lax.fori_loop(0, 4, drain_weights, 0)

    def drain_sums(step, carry):
        await_bytes(sums_kx.at[0], sum_send.at[step])
        return carry

    lax.fori_loop(0, KX_DEVICES + KY_DEVICES - 2, drain_sums, 0)
    for copy in halo_copies:
        copy.wait_send()
    homeward.wait_send()


def commutator_planes(coupled, state):
    coupled_real, coupled_imaginary = unpack(coupled)
    state_real, state_imaginary = unpack(state)

    def real_part(row, column):
        return product_sum(
            [
                term
                for middle in range(4)
                for term in (
                    (1.0, coupled_real[row][middle], state_real[middle][column]),
                    (-1.0, coupled_imaginary[row][middle], state_imaginary[middle][column]),
                    (-1.0, state_real[row][middle], coupled_real[middle][column]),
                    (1.0, state_imaginary[row][middle], coupled_imaginary[middle][column]),
                )
            ]
        )

    def imaginary_part(row, column):
        if row == column:
            return 2.0 * product_sum(
                [
                    term
                    for middle in range(4)
                    if middle != row
                    for term in (
                        (1.0, coupled_real[row][middle], state_imaginary[middle][column]),
                        (1.0, coupled_imaginary[row][middle], state_real[middle][column]),
                    )
                ]
            )
        return product_sum(
            [
                term
                for middle in range(4)
                for term in (
                    (1.0, coupled_real[row][middle], state_imaginary[middle][column]),
                    (1.0, coupled_imaginary[row][middle], state_real[middle][column]),
                    (-1.0, state_real[row][middle], coupled_imaginary[middle][column]),
                    (-1.0, state_imaginary[row][middle], coupled_real[middle][column]),
                )
            ]
        )

    return (
        [imaginary_part(band, band) for band in range(4)]
        + [imaginary_part(row, column) for row, column in BAND_PAIRS]
        + [-real_part(row, column) for row, column in BAND_PAIRS]
    )


def constant_tables():
    forward, backward = [], []
    for upper in range(2):
        table = kx_table(upper)
        for tables, values in ((forward, table), (backward, table.T)):
            high, low = split_table(values)
            tables.append(np.concatenate([high, high, low], axis=1))
    first, second, third = ky_tables()
    short = [np.concatenate([first, second]), np.concatenate([first.T, second.T])]
    long = [third, third.T]
    return (
        np.stack(forward),
        np.stack(backward),
        np.stack([np.stack(split_table(values)) for values in short]),
        np.stack([np.stack(split_table(values)) for values in long]),
        pick_table().astype(ml_dtypes.bfloat16),
    )


def section_body(packed_state_matrix, energies, dipole_x, dipole_y, interaction, driving_field):
    tables = [jnp.asarray(table) for table in constant_tables()]
    vmem = pl.BlockSpec(memory_space=pltpu.VMEM)
    smem = pl.BlockSpec(memory_space=pltpu.SMEM)
    anywhere = pl.BlockSpec(memory_space=pl.ANY)
    f32 = jnp.float32
    dma = pltpu.SemaphoreType.DMA
    plane_stack = (COMPONENTS, ROWS, COLUMNS)
    return pl.pallas_call(
        section_kernel,
        out_shape=(
            jax.ShapeDtypeStruct(plane_stack, f32),
            jax.ShapeDtypeStruct((2,), f32),
        ),
        in_specs=[vmem] * 5 + [smem] + [vmem] * 2 + [anywhere] * 3,
        out_specs=(vmem, smem),
        scratch_shapes=[
            pltpu.VMEM((4, 128, 128), f32),
            pltpu.VMEM(plane_stack, f32),
            pltpu.VMEM((2, 32, COLUMNS), f32),
            pltpu.VMEM((2, 32, COLUMNS), f32),
            pltpu.VMEM((ROWS, COLUMNS), f32),
            pltpu.VMEM((2, ROWS, COLUMNS), f32),
            pltpu.VMEM((COMPONENTS, 48, COLUMNS), f32),
            pltpu.VMEM((16, 640), f32),
            pltpu.VMEM((32, 640), f32),
            pltpu.VMEM((8, 640), f32),
            pltpu.VMEM((128, 512), f32),
            pltpu.VMEM((64, 512), f32),
            pltpu.VMEM((128, 512), f32),
            pltpu.VMEM((4, 128, 128), f32),
            pltpu.VMEM((KX_DEVICES, 8, COLUMNS), f32),
            pltpu.VMEM((KY_DEVICES, 8, COLUMNS), f32),
            pltpu.VMEM(plane_stack, f32),
            pltpu.VMEM((2, 2, 512, 256), jnp.bfloat16),
            pltpu.VMEM((2, 2, 512, 512), jnp.bfloat16),
            pltpu.VMEM((1024, 640), jnp.bfloat16),
            dma((3,)),
            dma((16,)),
            dma((16,)),
            dma((4,)),
            dma((4,)),
            dma((4,)),
            dma((3,)),
            dma((2,)),
            dma((2,)),
            dma((16,)),
            dma((16,)),
            dma((10,)),
            dma((12,)),
        ],
        compiler_params=pltpu.CompilerParams(
            collective_id=0, has_side_effects=True, vmem_limit_bytes=40 * 1024 * 1024
        ),
        cost_estimate=pl.CostEstimate(flops=1_200_000_000, bytes_accessed=6_000_000, transcendentals=0),
    )(packed_state_matrix, energies, dipole_x, dipole_y, interaction, driving_field, *tables)


def solution(mesh):
    in_specs = (
        P(None, "kx", "ky"),
        P(None, "kx", "ky"),
        P(None, "kx", "ky"),
        P(None, "kx", "ky"),
        P("ky", None),
        P(),
    )
    out_specs = (P(None, "kx", "ky"), P())
    chosen = section_body if fits_section_kernel(mesh) else body
    return jax.shard_map(chosen, mesh=mesh, in_specs=in_specs, out_specs=out_specs, check_vma=False)
```

```python
from functools import partial
import math

import jax
import jax.numpy as jnp
import ml_dtypes
import numpy as np
from jax import lax
from jax.experimental import pallas as pl
from jax.experimental.pallas import tpu as pltpu
from jax.sharding import PartitionSpec as P

BAND_PAIRS = ((0, 1), (0, 2), (0, 3), (1, 2), (1, 3), (2, 3))
DEPHASING = 0.5
SHIELDING_LEVEL = 2.0
COUPLING = 40.0


def with_halo(array, sides, width):
    for axis, dim in sides:
        devices, length = (lax.axis_size(axis), array.shape[dim])
        up = [(i, (i + 1) % devices) for i in range(devices)]
        down = [(j, i) for i, j in up]
        last = lax.slice_in_dim(array, length - width, length, axis=dim)
        initial = lax.slice_in_dim(array, 0, width, axis=dim)
        before = lax.ppermute(last, axis, up)
        after = lax.ppermute(initial, axis, down)
        array = jnp.concatenate([before, array, after], axis=dim)
    return array


def unpack(packed):
    real_entries = []
    imaginary_entries = []
    for band_one in range(4):
        real_entries.append([None, None, None, None])
        imaginary_entries.append([None, None, None, None])
    for band_one in range(4):
        real_entries[band_one][band_one] = packed[band_one]
    for number, band_pair in enumerate(BAND_PAIRS):
        upper_band, lower_band = band_pair
        real_entries[upper_band][lower_band] = packed[4 + number]
        real_entries[lower_band][upper_band] = packed[4 + number]
        imaginary_entries[upper_band][lower_band] = packed[10 + number]
        imaginary_entries[lower_band][upper_band] = -packed[10 + number]
    return (real_entries, imaginary_entries)


def product_sum(terms):
    summed = None
    for factor, left_value, right_value in terms:
        if left_value is None or right_value is None:
            continue
        product = factor * left_value * right_value
        summed = product if summed is None else summed + product
    return summed


def commutator(coupled, packed_state_matrix):
    coupled_real, coupled_imaginary = unpack(coupled)
    state_real, state_imaginary = unpack(packed_state_matrix)

    def element(row_band, column_band):
        real_terms = []
        imaginary_terms = []
        for middle in range(4):
            real_terms.append(
                (1.0, coupled_real[row_band][middle], state_real[middle][column_band])
            )
            real_terms.append(
                (-1.0, coupled_imaginary[row_band][middle], state_imaginary[middle][column_band])
            )
            real_terms.append(
                (-1.0, state_real[row_band][middle], coupled_real[middle][column_band])
            )
            real_terms.append(
                (1.0, state_imaginary[row_band][middle], coupled_imaginary[middle][column_band])
            )
            imaginary_terms.append(
                (1.0, coupled_real[row_band][middle], state_imaginary[middle][column_band])
            )
            imaginary_terms.append(
                (1.0, coupled_imaginary[row_band][middle], state_real[middle][column_band])
            )
            imaginary_terms.append(
                (-1.0, state_real[row_band][middle], coupled_imaginary[middle][column_band])
            )
            imaginary_terms.append(
                (-1.0, state_imaginary[row_band][middle], coupled_real[middle][column_band])
            )
        return (product_sum(real_terms), product_sum(imaginary_terms))

    diagonal = []
    upper_real = []
    upper_imaginary = []
    for band_one in range(4):
        diagonal.append(element(band_one, band_one)[1])
    for upper_band, lower_band in BAND_PAIRS:
        real_value, imaginary_value = element(upper_band, lower_band)
        upper_real.append(imaginary_value)
        upper_imaginary.append(-real_value)
    return jnp.stack(diagonal + upper_real + upper_imaginary)


def slope_terms(
    packed_state_matrix,
    energies,
    self_energy,
    gradient_x,
    gradient_y,
    dipole_x,
    dipole_y,
    driving_field,
):
    field_x = driving_field[0]
    field_y = driving_field[1]
    coupled = jnp.concatenate(
        [energies + self_energy[0:4], self_energy[4:16] + field_x * dipole_x + field_y * dipole_y]
    )
    rotation = commutator(coupled, packed_state_matrix)
    drift = rotation + field_x * gradient_x + field_y * gradient_y
    return jnp.concatenate([drift[0:4], drift[4:16] - DEPHASING * packed_state_matrix[4:16]])


def angle_table(row_count, column_count, period, direction):
    row_index = lax.broadcasted_iota(jnp.int32, (row_count, column_count), 0)
    column_index = lax.broadcasted_iota(jnp.int32, (row_count, column_count), 1)
    phase_angle = (row_index * column_index % period).astype(jnp.float32) * (
        direction * 2.0 * math.pi / period
    )
    return (jnp.cos(phase_angle), jnp.sin(phase_angle))


def complex_contract(einsum_form, data_real, data_imaginary, table_real, table_imaginary):
    contract = partial(
        jnp.einsum, precision=lax.Precision.HIGHEST, preferred_element_type=jnp.float32
    )
    if data_imaginary is None:
        return (
            contract(einsum_form, data_real, table_real),
            contract(einsum_form, data_real, table_imaginary),
        )
    real_out = contract(einsum_form, data_real, table_real) - contract(
        einsum_form, data_imaginary, table_imaginary
    )
    imaginary_out = contract(einsum_form, data_real, table_imaginary) + contract(
        einsum_form, data_imaginary, table_real
    )
    return (real_out, imaginary_out)


def transform(data_real, data_imaginary, direction, along_last):
    length = data_real.shape[-1] if along_last else data_real.shape[-2]
    outer_size = 16
    inner_size = length // outer_size
    outer_cosine, outer_sine = angle_table(outer_size, outer_size, outer_size, direction)
    twist_cosine, twist_sine = angle_table(outer_size, inner_size, length, direction)
    inner_cosine, inner_sine = angle_table(inner_size, inner_size, inner_size, direction)
    if along_last:
        split_shape = data_real.shape[:-1] + (outer_size, inner_size)
        first_form = "...aq,ab->...bq"
        second_form = "...bq,qc->...cb"
    else:
        split_shape = data_real.shape[:-2] + (outer_size, inner_size, data_real.shape[-1])
        first_form = "...aqt,ab->...bqt"
        second_form = "...bqt,qc->...cbt"
        twist_cosine = twist_cosine[:, :, None]
        twist_sine = twist_sine[:, :, None]
    part_real = data_real.reshape(split_shape)
    part_imaginary = None if data_imaginary is None else data_imaginary.reshape(split_shape)
    section_real, section_imaginary = complex_contract(
        first_form, part_real, part_imaginary, outer_cosine, outer_sine
    )
    turned_real = section_real * twist_cosine - section_imaginary * twist_sine
    turned_imaginary = section_real * twist_sine + section_imaginary * twist_cosine
    final_real, final_imaginary = complex_contract(
        second_form, turned_real, turned_imaginary, inner_cosine, inner_sine
    )
    return (final_real.reshape(data_real.shape), final_imaginary.reshape(data_real.shape))


def convolve(source, interaction, primitive_tile_total):
    along_kx = lax.all_to_all(source, "kx", split_axis=0, concat_axis=1, tiled=True)
    broad_nonimaginary, wide_imaginary = transform(along_kx, None, -1.0, False)
    joined = jnp.stack([broad_nonimaginary, wide_imaginary])
    along_ky = lax.all_to_all(joined, "ky", split_axis=2, concat_axis=3, tiled=True)
    line_real, line_imaginary = transform(along_ky[0], along_ky[1], -1.0, True)
    line_real, line_imaginary = transform(
        line_real * interaction, line_imaginary * interaction, 1.0, True
    )
    returned = lax.all_to_all(
        jnp.stack([line_real, line_imaginary]), "ky", split_axis=3, concat_axis=2, tiled=True
    )
    final_real, final_imaginary = transform(returned[0], returned[1], 1.0, False)
    normalizer = 1.0 / primitive_tile_total
    return lax.all_to_all(final_real * normalizer, "kx", split_axis=1, concat_axis=0, tiled=True)


def collect_moments(local_sums, primitive_tile_total):
    return lax.psum(local_sums, ("kx", "ky")) / primitive_tile_total


def body(packed_state_matrix, energies, dipole_x, dipole_y, interaction, driving_field):
    rows_local = packed_state_matrix.shape[1]
    columns_local = packed_state_matrix.shape[2]
    primitive_tile_total = rows_local * columns_local * lax.axis_size("kx") * lax.axis_size("ky")
    stacked = jnp.concatenate([packed_state_matrix, energies])
    padded = with_halo(stacked, (("kx", 1), ("ky", 2)), 2)
    column_core = padded[:, :, 2:-2]
    row_core = padded[:, 2:-2, :]
    gradient_x = (
        8.0 * (column_core[:, 3:-1] - column_core[:, 1:-3])
        - (column_core[:, 4:] - column_core[:, :-4])
    ) / 12.0
    gradient_y = (
        8.0 * (row_core[:, :, 3:-1] - row_core[:, :, 1:-3])
        - (row_core[:, :, 4:] - row_core[:, :, :-4])
    ) / 12.0
    populations = packed_state_matrix[0:4]
    local_sums = jnp.stack(
        [
            jnp.sum(packed_state_matrix[2] + packed_state_matrix[3]),
            jnp.sum(gradient_x[16:20] * populations),
            jnp.sum(gradient_y[16:20] * populations),
        ]
    )
    totals = collect_moments(local_sums, primitive_tile_total)
    shielding_multiplier = 1.0 / (1.0 + SHIELDING_LEVEL * totals[0])
    self_energy = -convolve(
        packed_state_matrix * shielding_multiplier, interaction, primitive_tile_total
    )
    section_slope = slope_terms(
        packed_state_matrix,
        energies,
        self_energy,
        gradient_x[0:16],
        gradient_y[0:16],
        dipole_x,
        dipole_y,
        driving_field,
    )
    field_next = driving_field - COUPLING * totals[1:3]
    return (section_slope, field_next)


def split_table(values):
    high = values.astype(ml_dtypes.bfloat16)
    low = (values - high.astype(np.float64)).astype(ml_dtypes.bfloat16)
    return high, low


def kx_table(upper):
    length = 128
    x = np.arange(length)
    rows = []
    for half in range(2):
        positions = np.arange(32 * half, 32 * half + 32)
        if upper:
            orders = 16 * (positions // 16) + 16 - positions % 16
        else:
            orders = positions
        cosine = np.cos(2 * np.pi * (np.outer(orders, x) % length) / length)
        sine = np.sin(2 * np.pi * (np.outer(orders, x) % length) / length)
        cosine *= np.where((orders == 0) | (orders == 64), 1.0, np.sqrt(2.0))[:, None]
        sine *= np.sqrt(2.0)
        for at, order in enumerate(orders):
            if not upper and order == 0:
                sine[at] = np.where(x % 2 == 0, 1.0, -1.0)
            if upper and order == 64:
                sine[at] = 1.0
        rows += [cosine, sine]
    return np.concatenate(rows) / np.sqrt(length)


def ky_tables():
    length = 1024
    k = np.arange(512)[:, None]

    def waves(orders, reach):
        angle = 2 * np.pi * (k[:reach] * orders[None, :] % length) / length
        return np.cos(angle), np.sin(angle)

    m = np.arange(128)
    scale = np.sqrt(2.0 / length)
    cosine, sine = waves(4 * m, 256)
    cosine, sine = cosine * scale, sine * scale
    cosine[:, 0] = np.sqrt(1.0 / length)
    sine[:, 0] = np.where(np.arange(256) % 2 == 0, 1.0, -1.0) * np.sqrt(1.0 / length)
    first = np.concatenate([cosine, sine], axis=1)
    cosine, sine = waves(4 * m + 2, 256)
    second = np.concatenate([cosine, sine], axis=1) * scale
    cosine, sine = waves(4 * np.arange(256) + 1, 512)
    third = np.concatenate([cosine, sine], axis=1) * scale
    return first, second, third


def pick_table():
    m = np.arange(128)
    wanted = np.concatenate([4 * m, 4 * m + 2, 4 * np.arange(256) + 1, np.full(128, 512)])
    table = np.zeros((1024, 640))
    table[wanted, np.arange(640)] = 1.0
    return table


MESH = pl.DeviceIdType.MESH
COMPONENTS = 16
ROWS, COLUMNS = 32, 128
KX_DEVICES, KY_DEVICES = 4, 8


def fits_section_kernel(mesh):
    return (mesh.shape["kx"], mesh.shape["ky"]) == (KX_DEVICES, KY_DEVICES)


def bf16_parts(values):
    high = values.astype(jnp.bfloat16)
    low = (values - high.astype(jnp.float32)).astype(jnp.bfloat16)
    return high, low


def matmul(left, right):
    return jnp.dot(left, right, preferred_element_type=jnp.float32)


def rows_by_table(values, table_high, table_low):
    count = values.shape[0]
    high, low = bf16_parts(values)
    both = matmul(jnp.concatenate([high, low], axis=0), table_high)
    return both[:count] + both[count:] + matmul(high, table_low)


def table_by_columns(table, values):
    high, low = bf16_parts(values)
    return matmul(table, jnp.concatenate([high, low, high], axis=0))


def section_kernel(
    rho_far, energies_far, dipole_x_far, dipole_y_far, interaction_far, field,
    kx_forward_far, kx_back_far, ky_short, ky_long, pick,
    out, field_out,
    rho, energies, dipole_x, dipole_y, interaction, kx_forward, kx_back,
    lines, conv, halo_out, halo_in, columns_out, columns_in, extended,
    weights_own, weights, weight_special, turned, turned_in, back, final,
    sums_kx, sums_ky, static_part,
    short_table, long_table, pick_table_vmem,
    table_sem, send_sem, line_sem, halo_send, halo_recv, weight_send, weight_recv,
    pair_send, pair_recv, return_send, return_recv, sum_send, sum_recv,
):
    i = lax.axis_index("kx")
    j = lax.axis_index("ky")
    chip_y = i // 2
    half = i % 2
    upper = j // 4
    component = chip_y * 8 + j

    fetches = [
        pltpu.make_async_copy(source, target, table_sem.at[number])
        for number, (source, target) in enumerate(
            (
                (rho_far, rho),
                (interaction_far, interaction),
                (pick, pick_table_vmem),
                (energies_far, energies),
                (dipole_x_far, dipole_x),
                (dipole_y_far, dipole_y),
                (kx_forward_far, kx_forward),
                (ky_short, short_table),
                (ky_long, long_table),
                (kx_back_far, kx_back),
            )
        )
    ]
    for fetch in fetches:
        fetch.start()

    barrier = pltpu.get_barrier_semaphore()

    def greet(device, carry):
        @pl.when(device != i * KY_DEVICES + j)
        def _():
            pl.semaphore_signal(
                barrier, inc=1, device_id=(device // KY_DEVICES, device % KY_DEVICES), device_id_type=MESH
            )

        return carry

    lax.fori_loop(0, KX_DEVICES * KY_DEVICES, greet, 0)

    def remote(source, target, send, receive, device):
        return pltpu.make_async_remote_copy(
            src_ref=source, dst_ref=target, send_sem=send, recv_sem=receive,
            device_id=device, device_id_type=MESH,
        )

    def await_bytes(ref, semaphore):
        pltpu.make_async_copy(ref, ref, semaphore).wait()

    fetches[0].wait()
    lane = lax.broadcasted_iota(jnp.int32, (ROWS, COLUMNS), 1)
    packed_columns = jnp.zeros((ROWS, COLUMNS), jnp.float32)
    for c in range(COMPONENTS):
        plane = rho[c]
        halo_out[0, 2 * c : 2 * c + 2, :] = plane[0:2]
        halo_out[1, 2 * c : 2 * c + 2, :] = plane[ROWS - 2 : ROWS]
        first = pltpu.roll(plane, 2 * c, 1) if c else plane
        last = pltpu.roll(plane, 66 + 2 * c, 1)
        packed_columns = jnp.where((lane // 2) == c, first, packed_columns)
        packed_columns = jnp.where((lane // 2) == 32 + c, last, packed_columns)
        extended[c, 8 : 8 + ROWS, :] = plane
    columns_out[...] = packed_columns

    pl.semaphore_wait(barrier, KX_DEVICES * KY_DEVICES - 1)

    def forward_target(step):
        c = (component + 1 + step) % COMPONENTS
        return c, 2 * (c // 8) + upper, c % 8

    def send_forward(step, carry):
        c, target_i, target_j = forward_target(step)
        slot = i * 4 + j % 4
        target = lines.at[j % 4, pl.ds(pl.multiple_of(ROWS * i, ROWS), ROWS), :]
        own = (target_i == i) & (target_j == j)

        @pl.when(jnp.logical_not(own))
        def _():
            remote(rho.at[c], target, send_sem.at[step], line_sem.at[slot], (target_i, target_j)).start()

        @pl.when(own)
        def _():
            pltpu.make_async_copy(rho.at[c], target, line_sem.at[slot]).start()

        return carry

    lax.fori_loop(0, COMPONENTS, send_forward, 0)

    before_i, after_i = (i + KX_DEVICES - 1) % KX_DEVICES, (i + 1) % KX_DEVICES
    before_j, after_j = (j + KY_DEVICES - 1) % KY_DEVICES, (j + 1) % KY_DEVICES
    halo_copies = [
        remote(halo_out.at[0], halo_in.at[1], halo_send.at[0], halo_recv.at[0], (before_i, j)),
        remote(halo_out.at[1], halo_in.at[0], halo_send.at[1], halo_recv.at[1], (after_i, j)),
        remote(columns_out, columns_in.at[1], halo_send.at[2], halo_recv.at[2], (i, before_j)),
        remote(columns_out, columns_in.at[0], halo_send.at[3], halo_recv.at[3], (i, after_j)),
    ]
    for copy in halo_copies:
        copy.start()

    fetches[1].wait()
    fetches[2].wait()
    high = interaction[...].astype(jnp.bfloat16)
    rest = interaction[...] - high.astype(jnp.float32)
    middle = rest.astype(jnp.bfloat16)
    low = (rest - middle.astype(jnp.float32)).astype(jnp.bfloat16)
    picked = matmul(jnp.concatenate([high, middle, low], axis=0), pick_table_vmem[...])
    weights_own[...] = picked[0:16] + picked[16:32] + picked[32:48]

    block = jnp.where(upper == 0, j, 7 - j)
    sends_weights = half == block // 2
    sends_special = ((j == 4) & (half == 0)) | ((j == 0) & (half == 1))
    special_group = 1 - upper

    def send_weights(step, carry):
        target_j = 4 * upper + step
        target = weights.at[pl.ds(pl.multiple_of(16 * (block % 2), 16), 16), :]

        @pl.when(sends_weights & (target_j != j))
        def _():
            remote(
                weights_own, target, weight_send.at[step], weight_recv.at[block % 2], (i, target_j)
            ).start()

        @pl.when(sends_weights & (target_j == j))
        def _():
            pltpu.make_async_copy(weights_own, target, weight_recv.at[block % 2]).start()

        @pl.when(sends_special)
        def _():
            remote(
                weights_own.at[pl.ds(0, 8), :], weight_special, weight_send.at[step], weight_recv.at[2],
                (i, 4 * special_group + step),
            ).start()

        return carry

    lax.fori_loop(0, 4, send_weights, 0)

    for fetch in fetches[3:6]:
        fetch.wait()
    for copy in halo_copies:
        copy.wait_recv()
    field_x = field[0]
    field_y = field[1]
    left_columns = columns_in[0]
    right_columns = columns_in[1]
    carriers_part = jnp.zeros((ROWS, COLUMNS), jnp.float32)
    current_x_part = jnp.zeros((ROWS, COLUMNS), jnp.float32)
    current_y_part = jnp.zeros((ROWS, COLUMNS), jnp.float32)
    for c in range(COMPONENTS):
        extended[c, 6:8, :] = halo_in[0, 2 * c : 2 * c + 2, :]
        extended[c, 8 + ROWS : 10 + ROWS, :] = halo_in[1, 2 * c : 2 * c + 2, :]
        plane = rho[c]
        gradient_x = (
            8.0 * (extended[c, 9 : 9 + ROWS, :] - extended[c, 7 : 7 + ROWS, :])
            - (extended[c, 10 : 10 + ROWS, :] - extended[c, 6 : 6 + ROWS, :])
        ) * (1.0 / 12.0)
        ahead_edge = pltpu.roll(right_columns, (127 - 2 * c) % 128, 1)
        ahead_two_edge = pltpu.roll(right_columns, (126 - 2 * c) % 128, 1)
        behind_edge = pltpu.roll(left_columns, (63 - 2 * c) % 128, 1)
        behind_two_edge = pltpu.roll(left_columns, 64 - 2 * c, 1)
        ahead = jnp.where(lane >= 127, ahead_edge, pltpu.roll(plane, 127, 1))
        ahead_two = jnp.where(lane >= 126, ahead_two_edge, pltpu.roll(plane, 126, 1))
        behind = jnp.where(lane < 1, behind_edge, pltpu.roll(plane, 1, 1))
        behind_two = jnp.where(lane < 2, behind_two_edge, pltpu.roll(plane, 2, 1))
        gradient_y = (8.0 * (ahead - behind) - (ahead_two - behind_two)) * (1.0 / 12.0)
        drift = field_x * gradient_x + field_y * gradient_y
        if c < 4:
            current_x_part = current_x_part - energies[c] * gradient_x
            current_y_part = current_y_part - energies[c] * gradient_y
            static_part[c] = energies[c]
        else:
            drift = drift - DEPHASING * plane
            static_part[c] = field_x * dipole_x[c - 4] + field_y * dipole_y[c - 4]
        if c in (2, 3):
            carriers_part = carriers_part + plane
        out[c] = drift

    def lane_sums(part):
        folded = part[0:8] + part[8:16] + part[16:24] + part[24:32]
        return jnp.sum(folded, axis=0, keepdims=True)

    sums_kx[i] = jnp.concatenate(
        [
            lane_sums(carriers_part), lane_sums(current_x_part), lane_sums(current_y_part),
            jnp.zeros((5, COLUMNS), jnp.float32),
        ],
        axis=0,
    )

    def send_sums_kx(step, carry):
        target = (i + 1 + step) % KX_DEVICES
        remote(sums_kx.at[i], sums_kx.at[i], sum_send.at[step], sum_recv.at[i], (target, j)).start()
        return carry

    lax.fori_loop(0, KX_DEVICES - 1, send_sums_kx, 0)

    def await_line(slot, carry):
        await_bytes(
            lines.at[slot % 4, pl.ds(pl.multiple_of(ROWS * (slot // 4), ROWS), ROWS), :], line_sem.at[slot]
        )
        return carry

    lax.fori_loop(0, COMPONENTS, await_line, 0)
    fetches[6].wait()
    whole_lines = jnp.concatenate([lines[0], lines[1], lines[2], lines[3]], axis=1)
    turned[...] = table_by_columns(kx_forward[upper], whole_lines)

    own_rows = pl.ds(pl.multiple_of(64 * half, 64), 64)
    other_rows = pl.ds(pl.multiple_of(64 * (1 - half), 64), 64)
    partner = (2 * chip_y + 1 - half, j)
    outward = remote(turned.at[other_rows, :], turned_in, pair_send.at[0], pair_recv.at[0], partner)
    outward.start()

    def await_sums_kx(step, carry):
        source = (i + 1 + step) % KX_DEVICES
        await_bytes(sums_kx.at[source], sum_recv.at[source])
        return carry

    lax.fori_loop(0, KX_DEVICES - 1, await_sums_kx, 0)
    sums_ky[j] = (sums_kx[0] + sums_kx[1]) + (sums_kx[2] + sums_kx[3])

    def send_sums_ky(step, carry):
        target = (j + 1 + step) % KY_DEVICES
        remote(
            sums_ky.at[j], sums_ky.at[j], sum_send.at[3 + step], sum_recv.at[KX_DEVICES + j], (i, target)
        ).start()
        return carry

    lax.fori_loop(0, KY_DEVICES - 1, send_sums_ky, 0)

    await_bytes(weights.at[pl.ds(0, 16), :], weight_recv.at[0])
    await_bytes(weights.at[pl.ds(16, 16), :], weight_recv.at[1])

    @pl.when(half == upper)
    def _():
        await_bytes(weight_special, weight_recv.at[2])

    @pl.when(half != upper)
    def _():
        weight_special[...] = jnp.zeros_like(weight_special)

    fetches[7].wait()
    fetches[8].wait()
    weight_rows = weights[...]
    special = jnp.concatenate([weight_special[0:1, :]] * 32, axis=0)
    row_at = lax.broadcasted_iota(jnp.int32, (32, 640), 0)
    at_special = (row_at == 16 * upper) & (half == upper)
    weight_rows = jnp.concatenate([weight_rows, jnp.where(at_special, special, weight_rows)], axis=0)
    lane_at = lax.broadcasted_iota(jnp.int32, (64, 128), 1)
    weight_sine = jnp.where(lane_at == 0, weight_rows[:, 512:640], weight_rows[:, 0:128])
    weight_first = jnp.concatenate([weight_rows[:, 0:128], weight_sine], axis=1)
    weight_second = jnp.concatenate([weight_rows[:, 128:256]] * 2, axis=1)
    weight_third = jnp.concatenate([weight_rows[:, 256:512]] * 2, axis=1)

    outward.wait_recv()
    sign = jnp.where(half == 0, 1.0, -1.0)
    own = turned[own_rows, :]
    other = turned_in[...]
    even = own + other
    odd = sign * (own - other)
    first = rows_by_table(even[:, :256] + even[:, 256:], short_table[0, 0, :256], short_table[0, 1, :256])
    second = rows_by_table(even[:, :256] - even[:, 256:], short_table[0, 0, 256:], short_table[0, 1, 256:])
    third = rows_by_table(odd, long_table[0, 0], long_table[0, 1])
    first = rows_by_table(first * weight_first, short_table[1, 0, :256], short_table[1, 1, :256])
    second = rows_by_table(second * weight_second, short_table[1, 0, 256:], short_table[1, 1, 256:])
    odd = sign * rows_by_table(third * weight_third, long_table[1, 0], long_table[1, 1])
    even = jnp.concatenate([first + second, first - second], axis=1)
    outward.wait_send()
    turned[own_rows, :] = even - odd
    back[own_rows, :] = even + odd
    homeward = remote(turned.at[own_rows, :], back.at[own_rows, :], pair_send.at[1], pair_recv.at[1], partner)
    homeward.start()

    def await_sums_ky(step, carry):
        source = (j + 1 + step) % KY_DEVICES
        await_bytes(sums_ky.at[source], sum_recv.at[KX_DEVICES + source])
        return carry

    lax.fori_loop(0, KY_DEVICES - 1, await_sums_ky, 0)
    totals = sums_ky[0]
    for source in range(1, KY_DEVICES):
        totals = totals + sums_ky[source]
    point_total = ROWS * COLUMNS * KX_DEVICES * KY_DEVICES
    means = jnp.sum(totals, axis=1, keepdims=True) * (1.0 / point_total)
    screen = 1.0 / (1.0 + SHIELDING_LEVEL * means[0:1, :])
    field_out[0] = field_x - COUPLING * jnp.sum(means[1:2, :])
    field_out[1] = field_y - COUPLING * jnp.sum(means[2:3, :])

    await_bytes(back.at[other_rows, :], pair_recv.at[1])
    fetches[9].wait()
    convolved = table_by_columns(kx_back[upper], back[...])
    for quarter in range(4):
        final[quarter] = convolved[:, 128 * quarter : 128 * quarter + 128]

    def send_back(step, carry):
        slot = (4 * i + j % 4 + 1 + step) % 16
        target_i = slot // 4
        target_j = 4 * half + slot % 4
        source = final.at[slot % 4, pl.ds(pl.multiple_of(ROWS * target_i, ROWS), ROWS), :]
        own_target = (target_i == i) & (target_j == j)

        @pl.when(jnp.logical_not(own_target))
        def _():
            remote(
                source, conv.at[component], return_send.at[step], return_recv.at[component],
                (target_i, target_j),
            ).start()

        @pl.when(own_target)
        def _():
            pltpu.make_async_copy(source, conv.at[component], return_recv.at[component]).start()

        return carry

    lax.fori_loop(0, COMPONENTS, send_back, 0)

    def await_back(c, carry):
        await_bytes(conv.at[c], return_recv.at[c])
        return carry

    lax.fori_loop(0, COMPONENTS, await_back, 0)

    def rotate(group, carry):
        rows = pl.ds(pl.multiple_of(8 * group, 8), 8)
        coupled = [static_part[c, rows, :] - screen * conv[c, rows, :] for c in range(COMPONENTS)]
        state = [rho[c, rows, :] for c in range(COMPONENTS)]
        rotation = commutator_planes(coupled, state)
        for c in range(COMPONENTS):
            out[c, rows, :] = out[c, rows, :] + rotation[c]
        return carry

    lax.fori_loop(0, ROWS // 8, rotate, 0)

    def drain(step, carry):
        c, target_i, target_j = forward_target(step)

        @pl.when(jnp.logical_not((target_i == i) & (target_j == j)))
        def _():
            await_bytes(rho.at[c], send_sem.at[step])

        slot = (4 * i + j % 4 + 1 + step) % 16

        @pl.when(jnp.logical_not((slot // 4 == i) & (4 * half + slot % 4 == j)))
        def _():
            await_bytes(conv.at[component], return_send.at[step])

        return carry

    lax.fori_loop(0, COMPONENTS, drain, 0)

    def drain_weights(step, carry):
        @pl.when(sends_weights & (4 * upper + step != j))
        def _():
            await_bytes(weights_own, weight_send.at[step])

        @pl.when(sends_special)
        def _():
            await_bytes(weight_special, weight_send.at[step])

        return carry

    lax.fori_loop(0, 4, drain_weights, 0)

    def drain_sums(step, carry):
        await_bytes(sums_kx.at[0], sum_send.at[step])
        return carry

    lax.fori_loop(0, KX_DEVICES + KY_DEVICES - 2, drain_sums, 0)
    for copy in halo_copies:
        copy.wait_send()
    homeward.wait_send()


def commutator_planes(coupled, state):
    coupled_real, coupled_imaginary = unpack(coupled)
    state_real, state_imaginary = unpack(state)

    def real_part(row, column):
        return product_sum(
            [
                term
                for middle in range(4)
                for term in (
                    (1.0, coupled_real[row][middle], state_real[middle][column]),
                    (-1.0, coupled_imaginary[row][middle], state_imaginary[middle][column]),
                    (-1.0, state_real[row][middle], coupled_real[middle][column]),
                    (1.0, state_imaginary[row][middle], coupled_imaginary[middle][column]),
                )
            ]
        )

    def imaginary_part(row, column):
        if row == column:
            return 2.0 * product_sum(
                [
                    term
                    for middle in range(4)
                    if middle != row
                    for term in (
                        (1.0, coupled_real[row][middle], state_imaginary[middle][column]),
                        (1.0, coupled_imaginary[row][middle], state_real[middle][column]),
                    )
                ]
            )
        return product_sum(
            [
                term
                for middle in range(4)
                for term in (
                    (1.0, coupled_real[row][middle], state_imaginary[middle][column]),
                    (1.0, coupled_imaginary[row][middle], state_real[middle][column]),
                    (-1.0, state_real[row][middle], coupled_imaginary[middle][column]),
                    (-1.0, state_imaginary[row][middle], coupled_real[middle][column]),
                )
            ]
        )

    return (
        [imaginary_part(band, band) for band in range(4)]
        + [imaginary_part(row, column) for row, column in BAND_PAIRS]
        + [-real_part(row, column) for row, column in BAND_PAIRS]
    )


def constant_tables():
    forward, backward = [], []
    for upper in range(2):
        table = kx_table(upper)
        for tables, values in ((forward, table), (backward, table.T)):
            high, low = split_table(values)
            tables.append(np.concatenate([high, high, low], axis=1))
    first, second, third = ky_tables()
    short = [np.concatenate([first, second]), np.concatenate([first.T, second.T])]
    long = [third, third.T]
    return (
        np.stack(forward),
        np.stack(backward),
        np.stack([np.stack(split_table(values)) for values in short]),
        np.stack([np.stack(split_table(values)) for values in long]),
        pick_table().astype(ml_dtypes.bfloat16),
    )


def section_body(packed_state_matrix, energies, dipole_x, dipole_y, interaction, driving_field):
    tables = [jnp.asarray(table) for table in constant_tables()]
    vmem = pl.BlockSpec(memory_space=pltpu.VMEM)
    smem = pl.BlockSpec(memory_space=pltpu.SMEM)
    anywhere = pl.BlockSpec(memory_space=pl.ANY)
    f32 = jnp.float32
    dma = pltpu.SemaphoreType.DMA
    plane_stack = (COMPONENTS, ROWS, COLUMNS)
    return pl.pallas_call(
        section_kernel,
        out_shape=(
            jax.ShapeDtypeStruct(plane_stack, f32),
            jax.ShapeDtypeStruct((2,), f32),
        ),
        in_specs=[anywhere] * 5 + [smem] + [anywhere] * 5,
        out_specs=(vmem, smem),
        scratch_shapes=[
            pltpu.VMEM(plane_stack, f32),
            pltpu.VMEM((4, ROWS, COLUMNS), f32),
            pltpu.VMEM((12, ROWS, COLUMNS), f32),
            pltpu.VMEM((12, ROWS, COLUMNS), f32),
            pltpu.VMEM((16, 1024), f32),
            pltpu.VMEM((2, 128, 384), jnp.bfloat16),
            pltpu.VMEM((2, 128, 384), jnp.bfloat16),
            pltpu.VMEM((4, 128, 128), f32),
            pltpu.VMEM(plane_stack, f32),
            pltpu.VMEM((2, 32, COLUMNS), f32),
            pltpu.VMEM((2, 32, COLUMNS), f32),
            pltpu.VMEM((ROWS, COLUMNS), f32),
            pltpu.VMEM((2, ROWS, COLUMNS), f32),
            pltpu.VMEM((COMPONENTS, 48, COLUMNS), f32),
            pltpu.VMEM((16, 640), f32),
            pltpu.VMEM((32, 640), f32),
            pltpu.VMEM((8, 640), f32),
            pltpu.VMEM((128, 512), f32),
            pltpu.VMEM((64, 512), f32),
            pltpu.VMEM((128, 512), f32),
            pltpu.VMEM((4, 128, 128), f32),
            pltpu.VMEM((KX_DEVICES, 8, COLUMNS), f32),
            pltpu.VMEM((KY_DEVICES, 8, COLUMNS), f32),
            pltpu.VMEM(plane_stack, f32),
            pltpu.VMEM((2, 2, 512, 256), jnp.bfloat16),
            pltpu.VMEM((2, 2, 512, 512), jnp.bfloat16),
            pltpu.VMEM((1024, 640), jnp.bfloat16),
            dma((10,)),
            dma((16,)),
            dma((16,)),
            dma((4,)),
            dma((4,)),
            dma((4,)),
            dma((3,)),
            dma((2,)),
            dma((2,)),
            dma((16,)),
            dma((16,)),
            dma((10,)),
            dma((12,)),
        ],
        compiler_params=pltpu.CompilerParams(
            collective_id=0, has_side_effects=True, vmem_limit_bytes=64 * 1024 * 1024
        ),
        cost_estimate=pl.CostEstimate(flops=1_200_000_000, bytes_accessed=6_000_000, transcendentals=0),
    )(packed_state_matrix, energies, dipole_x, dipole_y, interaction, driving_field, *tables)


def solution(mesh):
    in_specs = (
        P(None, "kx", "ky"),
        P(None, "kx", "ky"),
        P(None, "kx", "ky"),
        P(None, "kx", "ky"),
        P("ky", None),
        P(),
    )
    out_specs = (P(None, "kx", "ky"), P())
    chosen = section_body if fits_section_kernel(mesh) else body
    return jax.shard_map(chosen, mesh=mesh, in_specs=in_specs, out_specs=out_specs, check_vma=False)
```

```python
from functools import partial
import math

import jax
import jax.numpy as jnp
import ml_dtypes
import numpy as np
from jax import lax
from jax.experimental import pallas as pl
from jax.experimental.pallas import tpu as pltpu
from jax.sharding import PartitionSpec as P

BAND_PAIRS = ((0, 1), (0, 2), (0, 3), (1, 2), (1, 3), (2, 3))
DEPHASING = 0.5
SHIELDING_LEVEL = 2.0
COUPLING = 40.0


def with_halo(array, sides, width):
    for axis, dim in sides:
        devices, length = (lax.axis_size(axis), array.shape[dim])
        up = [(i, (i + 1) % devices) for i in range(devices)]
        down = [(j, i) for i, j in up]
        last = lax.slice_in_dim(array, length - width, length, axis=dim)
        initial = lax.slice_in_dim(array, 0, width, axis=dim)
        before = lax.ppermute(last, axis, up)
        after = lax.ppermute(initial, axis, down)
        array = jnp.concatenate([before, array, after], axis=dim)
    return array


def unpack(packed):
    real_entries = []
    imaginary_entries = []
    for band_one in range(4):
        real_entries.append([None, None, None, None])
        imaginary_entries.append([None, None, None, None])
    for band_one in range(4):
        real_entries[band_one][band_one] = packed[band_one]
    for number, band_pair in enumerate(BAND_PAIRS):
        upper_band, lower_band = band_pair
        real_entries[upper_band][lower_band] = packed[4 + number]
        real_entries[lower_band][upper_band] = packed[4 + number]
        imaginary_entries[upper_band][lower_band] = packed[10 + number]
        imaginary_entries[lower_band][upper_band] = -packed[10 + number]
    return (real_entries, imaginary_entries)


def product_sum(terms):
    summed = None
    for factor, left_value, right_value in terms:
        if left_value is None or right_value is None:
            continue
        product = factor * left_value * right_value
        summed = product if summed is None else summed + product
    return summed


def commutator(coupled, packed_state_matrix):
    coupled_real, coupled_imaginary = unpack(coupled)
    state_real, state_imaginary = unpack(packed_state_matrix)

    def element(row_band, column_band):
        real_terms = []
        imaginary_terms = []
        for middle in range(4):
            real_terms.append(
                (1.0, coupled_real[row_band][middle], state_real[middle][column_band])
            )
            real_terms.append(
                (-1.0, coupled_imaginary[row_band][middle], state_imaginary[middle][column_band])
            )
            real_terms.append(
                (-1.0, state_real[row_band][middle], coupled_real[middle][column_band])
            )
            real_terms.append(
                (1.0, state_imaginary[row_band][middle], coupled_imaginary[middle][column_band])
            )
            imaginary_terms.append(
                (1.0, coupled_real[row_band][middle], state_imaginary[middle][column_band])
            )
            imaginary_terms.append(
                (1.0, coupled_imaginary[row_band][middle], state_real[middle][column_band])
            )
            imaginary_terms.append(
                (-1.0, state_real[row_band][middle], coupled_imaginary[middle][column_band])
            )
            imaginary_terms.append(
                (-1.0, state_imaginary[row_band][middle], coupled_real[middle][column_band])
            )
        return (product_sum(real_terms), product_sum(imaginary_terms))

    diagonal = []
    upper_real = []
    upper_imaginary = []
    for band_one in range(4):
        diagonal.append(element(band_one, band_one)[1])
    for upper_band, lower_band in BAND_PAIRS:
        real_value, imaginary_value = element(upper_band, lower_band)
        upper_real.append(imaginary_value)
        upper_imaginary.append(-real_value)
    return jnp.stack(diagonal + upper_real + upper_imaginary)


def slope_terms(
    packed_state_matrix,
    energies,
    self_energy,
    gradient_x,
    gradient_y,
    dipole_x,
    dipole_y,
    driving_field,
):
    field_x = driving_field[0]
    field_y = driving_field[1]
    coupled = jnp.concatenate(
        [energies + self_energy[0:4], self_energy[4:16] + field_x * dipole_x + field_y * dipole_y]
    )
    rotation = commutator(coupled, packed_state_matrix)
    drift = rotation + field_x * gradient_x + field_y * gradient_y
    return jnp.concatenate([drift[0:4], drift[4:16] - DEPHASING * packed_state_matrix[4:16]])


def angle_table(row_count, column_count, period, direction):
    row_index = lax.broadcasted_iota(jnp.int32, (row_count, column_count), 0)
    column_index = lax.broadcasted_iota(jnp.int32, (row_count, column_count), 1)
    phase_angle = (row_index * column_index % period).astype(jnp.float32) * (
        direction * 2.0 * math.pi / period
    )
    return (jnp.cos(phase_angle), jnp.sin(phase_angle))


def complex_contract(einsum_form, data_real, data_imaginary, table_real, table_imaginary):
    contract = partial(
        jnp.einsum, precision=lax.Precision.HIGHEST, preferred_element_type=jnp.float32
    )
    if data_imaginary is None:
        return (
            contract(einsum_form, data_real, table_real),
            contract(einsum_form, data_real, table_imaginary),
        )
    real_out = contract(einsum_form, data_real, table_real) - contract(
        einsum_form, data_imaginary, table_imaginary
    )
    imaginary_out = contract(einsum_form, data_real, table_imaginary) + contract(
        einsum_form, data_imaginary, table_real
    )
    return (real_out, imaginary_out)


def transform(data_real, data_imaginary, direction, along_last):
    length = data_real.shape[-1] if along_last else data_real.shape[-2]
    outer_size = 16
    inner_size = length // outer_size
    outer_cosine, outer_sine = angle_table(outer_size, outer_size, outer_size, direction)
    twist_cosine, twist_sine = angle_table(outer_size, inner_size, length, direction)
    inner_cosine, inner_sine = angle_table(inner_size, inner_size, inner_size, direction)
    if along_last:
        split_shape = data_real.shape[:-1] + (outer_size, inner_size)
        first_form = "...aq,ab->...bq"
        second_form = "...bq,qc->...cb"
    else:
        split_shape = data_real.shape[:-2] + (outer_size, inner_size, data_real.shape[-1])
        first_form = "...aqt,ab->...bqt"
        second_form = "...bqt,qc->...cbt"
        twist_cosine = twist_cosine[:, :, None]
        twist_sine = twist_sine[:, :, None]
    part_real = data_real.reshape(split_shape)
    part_imaginary = None if data_imaginary is None else data_imaginary.reshape(split_shape)
    section_real, section_imaginary = complex_contract(
        first_form, part_real, part_imaginary, outer_cosine, outer_sine
    )
    turned_real = section_real * twist_cosine - section_imaginary * twist_sine
    turned_imaginary = section_real * twist_sine + section_imaginary * twist_cosine
    final_real, final_imaginary = complex_contract(
        second_form, turned_real, turned_imaginary, inner_cosine, inner_sine
    )
    return (final_real.reshape(data_real.shape), final_imaginary.reshape(data_real.shape))


def convolve(source, interaction, primitive_tile_total):
    along_kx = lax.all_to_all(source, "kx", split_axis=0, concat_axis=1, tiled=True)
    broad_nonimaginary, wide_imaginary = transform(along_kx, None, -1.0, False)
    joined = jnp.stack([broad_nonimaginary, wide_imaginary])
    along_ky = lax.all_to_all(joined, "ky", split_axis=2, concat_axis=3, tiled=True)
    line_real, line_imaginary = transform(along_ky[0], along_ky[1], -1.0, True)
    line_real, line_imaginary = transform(
        line_real * interaction, line_imaginary * interaction, 1.0, True
    )
    returned = lax.all_to_all(
        jnp.stack([line_real, line_imaginary]), "ky", split_axis=3, concat_axis=2, tiled=True
    )
    final_real, final_imaginary = transform(returned[0], returned[1], 1.0, False)
    normalizer = 1.0 / primitive_tile_total
    return lax.all_to_all(final_real * normalizer, "kx", split_axis=1, concat_axis=0, tiled=True)


def collect_moments(local_sums, primitive_tile_total):
    return lax.psum(local_sums, ("kx", "ky")) / primitive_tile_total


def body(packed_state_matrix, energies, dipole_x, dipole_y, interaction, driving_field):
    rows_local = packed_state_matrix.shape[1]
    columns_local = packed_state_matrix.shape[2]
    primitive_tile_total = rows_local * columns_local * lax.axis_size("kx") * lax.axis_size("ky")
    stacked = jnp.concatenate([packed_state_matrix, energies])
    padded = with_halo(stacked, (("kx", 1), ("ky", 2)), 2)
    column_core = padded[:, :, 2:-2]
    row_core = padded[:, 2:-2, :]
    gradient_x = (
        8.0 * (column_core[:, 3:-1] - column_core[:, 1:-3])
        - (column_core[:, 4:] - column_core[:, :-4])
    ) / 12.0
    gradient_y = (
        8.0 * (row_core[:, :, 3:-1] - row_core[:, :, 1:-3])
        - (row_core[:, :, 4:] - row_core[:, :, :-4])
    ) / 12.0
    populations = packed_state_matrix[0:4]
    local_sums = jnp.stack(
        [
            jnp.sum(packed_state_matrix[2] + packed_state_matrix[3]),
            jnp.sum(gradient_x[16:20] * populations),
            jnp.sum(gradient_y[16:20] * populations),
        ]
    )
    totals = collect_moments(local_sums, primitive_tile_total)
    shielding_multiplier = 1.0 / (1.0 + SHIELDING_LEVEL * totals[0])
    self_energy = -convolve(
        packed_state_matrix * shielding_multiplier, interaction, primitive_tile_total
    )
    section_slope = slope_terms(
        packed_state_matrix,
        energies,
        self_energy,
        gradient_x[0:16],
        gradient_y[0:16],
        dipole_x,
        dipole_y,
        driving_field,
    )
    field_next = driving_field - COUPLING * totals[1:3]
    return (section_slope, field_next)


def split_table(values):
    high = values.astype(ml_dtypes.bfloat16)
    low = (values - high.astype(np.float64)).astype(ml_dtypes.bfloat16)
    return high, low


def kx_table(upper):
    length = 128
    x = np.arange(length)
    rows = []
    for half in range(2):
        positions = np.arange(32 * half, 32 * half + 32)
        if upper:
            orders = 16 * (positions // 16) + 16 - positions % 16
        else:
            orders = positions
        cosine = np.cos(2 * np.pi * (np.outer(orders, x) % length) / length)
        sine = np.sin(2 * np.pi * (np.outer(orders, x) % length) / length)
        cosine *= np.where((orders == 0) | (orders == 64), 1.0, np.sqrt(2.0))[:, None]
        sine *= np.sqrt(2.0)
        for at, order in enumerate(orders):
            if not upper and order == 0:
                sine[at] = np.where(x % 2 == 0, 1.0, -1.0)
            if upper and order == 64:
                sine[at] = 1.0
        rows += [cosine, sine]
    return np.concatenate(rows) / np.sqrt(length)


def ky_tables():
    length = 1024
    k = np.arange(512)[:, None]

    def waves(orders, reach):
        angle = 2 * np.pi * (k[:reach] * orders[None, :] % length) / length
        return np.cos(angle), np.sin(angle)

    m = np.arange(128)
    scale = np.sqrt(2.0 / length)
    cosine, sine = waves(4 * m, 256)
    cosine, sine = cosine * scale, sine * scale
    cosine[:, 0] = np.sqrt(1.0 / length)
    sine[:, 0] = np.where(np.arange(256) % 2 == 0, 1.0, -1.0) * np.sqrt(1.0 / length)
    first = np.concatenate([cosine, sine], axis=1)
    cosine, sine = waves(4 * m + 2, 256)
    second = np.concatenate([cosine, sine], axis=1) * scale
    cosine, sine = waves(4 * np.arange(256) + 1, 512)
    third = np.concatenate([cosine, sine], axis=1) * scale
    return first, second, third


def pick_table():
    m = np.arange(128)
    wanted = np.concatenate([4 * m, 4 * m + 2, 4 * np.arange(256) + 1, np.full(128, 512)])
    table = np.zeros((1024, 640))
    table[wanted, np.arange(640)] = 1.0
    return table


MESH = pl.DeviceIdType.MESH
COMPONENTS = 16
ROWS, COLUMNS = 32, 128
KX_DEVICES, KY_DEVICES = 4, 8


def fits_section_kernel(mesh):
    return (mesh.shape["kx"], mesh.shape["ky"]) == (KX_DEVICES, KY_DEVICES)


def bf16_parts(values):
    high = values.astype(jnp.bfloat16)
    low = (values - high.astype(jnp.float32)).astype(jnp.bfloat16)
    return high, low


def matmul(left, right):
    return jnp.dot(left, right, preferred_element_type=jnp.float32)


def rows_by_table(values, table_high, table_low):
    count = values.shape[0]
    high, low = bf16_parts(values)
    both = matmul(jnp.concatenate([high, low], axis=0), table_high)
    return both[:count] + both[count:] + matmul(high, table_low)


def table_by_columns(table, values):
    high, low = bf16_parts(values)
    return matmul(table, jnp.concatenate([high, low, high], axis=0))


def section_kernel(
    rho_far, energies_far, dipole_x_far, dipole_y_far, interaction_far, field,
    kx_forward_far, kx_back_far, ky_short, ky_long, pick,
    out, field_out,
    rho, energies, dipole_x, dipole_y, interaction, kx_forward, kx_back,
    lines, conv, halo_out, halo_in, columns_out, columns_in, extended,
    weights_own, weights, weight_special, turned, turned_in, back_out, back_in, final, leaving,
    sums_kx, sums_ky, static_part,
    short_table, long_table, pick_table_vmem,
    table_sem, send_sem, line_sem, halo_send, halo_recv, weight_send, weight_recv,
    pair_send, pair_recv, return_send, return_recv, sum_send, sum_recv,
):
    i = lax.axis_index("kx")
    j = lax.axis_index("ky")
    chip_y = i // 2
    half = i % 2
    upper = j // 4
    place_z = j // 2
    parity = j % 2
    component = chip_y * 8 + j

    fetches = [
        pltpu.make_async_copy(source, target, table_sem.at[number])
        for number, (source, target) in enumerate(
            (
                (rho_far, rho),
                (interaction_far, interaction),
                (pick, pick_table_vmem),
                (energies_far, energies),
                (dipole_x_far, dipole_x),
                (dipole_y_far, dipole_y),
                (kx_forward_far, kx_forward),
                (ky_short, short_table),
                (ky_long, long_table),
                (kx_back_far, kx_back),
            )
        )
    ]
    for fetch in fetches:
        fetch.start()

    barrier = pltpu.get_barrier_semaphore()

    def greet(device, carry):
        @pl.when(device != i * KY_DEVICES + j)
        def _():
            pl.semaphore_signal(
                barrier, inc=1, device_id=(device // KY_DEVICES, device % KY_DEVICES), device_id_type=MESH
            )

        return carry

    lax.fori_loop(0, KX_DEVICES * KY_DEVICES, greet, 0)

    def remote(source, target, send, receive, device):
        return pltpu.make_async_remote_copy(
            src_ref=source, dst_ref=target, send_sem=send, recv_sem=receive,
            device_id=device, device_id_type=MESH,
        )

    def await_bytes(ref, semaphore):
        pltpu.make_async_copy(ref, ref, semaphore).wait()

    pl.semaphore_wait(barrier, KX_DEVICES * KY_DEVICES - 1)

    def toward(step):
        across = (step + 1) % 2
        number = jnp.where(across == 1, step // 2, 7 - step // 2)
        target_z = 2 * ((place_z // 2 + across) % 2) + (place_z + number) % 2
        target_x = (parity + number // 2) % 2
        target_y = (chip_y + number // 4) % 2
        return target_y, 2 * target_z + target_x

    def forward_target(step):
        target_y, target_j = toward(step)
        return 8 * target_y + target_j, 2 * target_y + parity, target_j

    def send_forward(step, carry):
        c, target_i, target_j = forward_target(step)
        slot = i * 4 + place_z
        target = lines.at[place_z, pl.ds(pl.multiple_of(ROWS * i, ROWS), ROWS), :]
        own = (target_i == i) & (target_j == j)

        @pl.when(jnp.logical_not(own))
        def _():
            remote(rho_far.at[c], target, send_sem.at[step], line_sem.at[slot], (target_i, target_j)).start()

        @pl.when(own)
        def _():
            pltpu.make_async_copy(rho_far.at[c], target, line_sem.at[slot]).start()

        return carry

    lax.fori_loop(0, COMPONENTS, send_forward, 0)

    fetches[0].wait()
    lane = lax.broadcasted_iota(jnp.int32, (ROWS, COLUMNS), 1)
    packed_columns = jnp.zeros((ROWS, COLUMNS), jnp.float32)
    for c in range(COMPONENTS):
        plane = rho[c]
        halo_out[0, 2 * c : 2 * c + 2, :] = plane[0:2]
        halo_out[1, 2 * c : 2 * c + 2, :] = plane[ROWS - 2 : ROWS]
        first = pltpu.roll(plane, 2 * c, 1) if c else plane
        last = pltpu.roll(plane, 66 + 2 * c, 1)
        packed_columns = jnp.where((lane // 2) == c, first, packed_columns)
        packed_columns = jnp.where((lane // 2) == 32 + c, last, packed_columns)
        extended[c, 8 : 8 + ROWS, :] = plane
    columns_out[...] = packed_columns

    before_i, after_i = (i + KX_DEVICES - 1) % KX_DEVICES, (i + 1) % KX_DEVICES
    before_j, after_j = (j + KY_DEVICES - 1) % KY_DEVICES, (j + 1) % KY_DEVICES
    halo_copies = [
        remote(halo_out.at[0], halo_in.at[1], halo_send.at[0], halo_recv.at[0], (before_i, j)),
        remote(halo_out.at[1], halo_in.at[0], halo_send.at[1], halo_recv.at[1], (after_i, j)),
        remote(columns_out, columns_in.at[1], halo_send.at[2], halo_recv.at[2], (i, before_j)),
        remote(columns_out, columns_in.at[0], halo_send.at[3], halo_recv.at[3], (i, after_j)),
    ]
    for copy in halo_copies:
        copy.start()

    fetches[1].wait()
    fetches[2].wait()
    high = interaction[...].astype(jnp.bfloat16)
    rest = interaction[...] - high.astype(jnp.float32)
    middle = rest.astype(jnp.bfloat16)
    low = (rest - middle.astype(jnp.float32)).astype(jnp.bfloat16)
    picked = matmul(jnp.concatenate([high, middle, low], axis=0), pick_table_vmem[...])
    weights_own[...] = picked[0:16] + picked[16:32] + picked[32:48]

    block = jnp.where(upper == 0, j, 7 - j)
    sends_weights = half == block // 2
    sends_special = ((j == 4) & (half == 0)) | ((j == 0) & (half == 1))
    special_group = 1 - upper

    def send_weights(step, carry):
        target_j = 4 * upper + step
        target = weights.at[pl.ds(pl.multiple_of(16 * (block % 2), 16), 16), :]

        @pl.when(sends_weights & (target_j != j))
        def _():
            remote(
                weights_own, target, weight_send.at[step], weight_recv.at[block % 2], (i, target_j)
            ).start()

        @pl.when(sends_weights & (target_j == j))
        def _():
            pltpu.make_async_copy(weights_own, target, weight_recv.at[block % 2]).start()

        @pl.when(sends_special)
        def _():
            remote(
                weights_own.at[pl.ds(0, 8), :], weight_special, weight_send.at[step], weight_recv.at[2],
                (i, 4 * special_group + step),
            ).start()

        return carry

    lax.fori_loop(0, 4, send_weights, 0)

    for fetch in fetches[3:6]:
        fetch.wait()
    for copy in halo_copies:
        copy.wait_recv()
    field_x = field[0]
    field_y = field[1]
    left_columns = columns_in[0]
    right_columns = columns_in[1]
    carriers_part = jnp.zeros((ROWS, COLUMNS), jnp.float32)
    current_x_part = jnp.zeros((ROWS, COLUMNS), jnp.float32)
    current_y_part = jnp.zeros((ROWS, COLUMNS), jnp.float32)
    for c in range(COMPONENTS):
        extended[c, 6:8, :] = halo_in[0, 2 * c : 2 * c + 2, :]
        extended[c, 8 + ROWS : 10 + ROWS, :] = halo_in[1, 2 * c : 2 * c + 2, :]
        plane = rho[c]
        gradient_x = (
            8.0 * (extended[c, 9 : 9 + ROWS, :] - extended[c, 7 : 7 + ROWS, :])
            - (extended[c, 10 : 10 + ROWS, :] - extended[c, 6 : 6 + ROWS, :])
        ) * (1.0 / 12.0)
        ahead_edge = pltpu.roll(right_columns, (127 - 2 * c) % 128, 1)
        ahead_two_edge = pltpu.roll(right_columns, (126 - 2 * c) % 128, 1)
        behind_edge = pltpu.roll(left_columns, (63 - 2 * c) % 128, 1)
        behind_two_edge = pltpu.roll(left_columns, 64 - 2 * c, 1)
        ahead = jnp.where(lane >= 127, ahead_edge, pltpu.roll(plane, 127, 1))
        ahead_two = jnp.where(lane >= 126, ahead_two_edge, pltpu.roll(plane, 126, 1))
        behind = jnp.where(lane < 1, behind_edge, pltpu.roll(plane, 1, 1))
        behind_two = jnp.where(lane < 2, behind_two_edge, pltpu.roll(plane, 2, 1))
        gradient_y = (8.0 * (ahead - behind) - (ahead_two - behind_two)) * (1.0 / 12.0)
        drift = field_x * gradient_x + field_y * gradient_y
        if c < 4:
            current_x_part = current_x_part - energies[c] * gradient_x
            current_y_part = current_y_part - energies[c] * gradient_y
            static_part[c] = energies[c]
        else:
            drift = drift - DEPHASING * plane
            static_part[c] = field_x * dipole_x[c - 4] + field_y * dipole_y[c - 4]
        if c in (2, 3):
            carriers_part = carriers_part + plane
        out[c] = drift

    def lane_sums(part):
        folded = part[0:8] + part[8:16] + part[16:24] + part[24:32]
        return jnp.sum(folded, axis=0, keepdims=True)

    sums_kx[i] = jnp.concatenate(
        [
            lane_sums(carriers_part), lane_sums(current_x_part), lane_sums(current_y_part),
            jnp.zeros((5, COLUMNS), jnp.float32),
        ],
        axis=0,
    )

    def send_sums_kx(step, carry):
        target = (i + 1 + step) % KX_DEVICES
        remote(sums_kx.at[i], sums_kx.at[i], sum_send.at[step], sum_recv.at[i], (target, j)).start()
        return carry

    lax.fori_loop(0, KX_DEVICES - 1, send_sums_kx, 0)

    own_rows = pl.ds(pl.multiple_of(64 * half, 64), 64)
    other_rows = pl.ds(pl.multiple_of(64 * (1 - half), 64), 64)
    partner = (2 * chip_y + 1 - half, j)
    fetches[6].wait()

    def quarter_at(step):
        return 2 * ((place_z // 2 + step // 2) % 2) + (place_z + step) % 2

    def pair_copy(quarter):
        return remote(
            turned.at[quarter, other_rows, :], turned_in.at[quarter], pair_send.at[quarter],
            pair_recv.at[quarter], partner,
        )

    def turn_quarter(step, carry):
        quarter = quarter_at(step)
        for source in range(KX_DEVICES):
            await_bytes(
                lines.at[quarter, pl.ds(ROWS * source, ROWS), :], line_sem.at[4 * source + quarter]
            )
        turned[quarter] = table_by_columns(kx_forward[upper], lines[quarter])
        pair_copy(quarter).start()
        return carry

    lax.fori_loop(0, 4, turn_quarter, 0)

    def await_sums_kx(step, carry):
        source = (i + 1 + step) % KX_DEVICES
        await_bytes(sums_kx.at[source], sum_recv.at[source])
        return carry

    lax.fori_loop(0, KX_DEVICES - 1, await_sums_kx, 0)
    sums_ky[j] = (sums_kx[0] + sums_kx[1]) + (sums_kx[2] + sums_kx[3])

    def send_sums_ky(step, carry):
        target = (j + 1 + step) % KY_DEVICES
        remote(
            sums_ky.at[j], sums_ky.at[j], sum_send.at[3 + step], sum_recv.at[KX_DEVICES + j], (i, target)
        ).start()
        return carry

    lax.fori_loop(0, KY_DEVICES - 1, send_sums_ky, 0)

    await_bytes(weights.at[pl.ds(0, 16), :], weight_recv.at[0])
    await_bytes(weights.at[pl.ds(16, 16), :], weight_recv.at[1])

    @pl.when(half == upper)
    def _():
        await_bytes(weight_special, weight_recv.at[2])

    @pl.when(half != upper)
    def _():
        weight_special[...] = jnp.zeros_like(weight_special)

    fetches[7].wait()
    fetches[8].wait()
    weight_rows = weights[...]
    special = jnp.concatenate([weight_special[0:1, :]] * 32, axis=0)
    row_at = lax.broadcasted_iota(jnp.int32, (32, 640), 0)
    at_special = (row_at == 16 * upper) & (half == upper)
    weight_rows = jnp.concatenate([weight_rows, jnp.where(at_special, special, weight_rows)], axis=0)
    lane_at = lax.broadcasted_iota(jnp.int32, (64, 128), 1)
    weight_sine = jnp.where(lane_at == 0, weight_rows[:, 512:640], weight_rows[:, 0:128])
    weight_first = jnp.concatenate([weight_rows[:, 0:128], weight_sine], axis=1)
    weight_second = jnp.concatenate([weight_rows[:, 128:256]] * 2, axis=1)
    weight_third = jnp.concatenate([weight_rows[:, 256:512]] * 2, axis=1)

    for quarter in range(4):
        await_bytes(turned_in.at[quarter], pair_recv.at[quarter])
    is_first = half == 0
    blocks = []
    for quarter in range(4):
        own = turned[quarter, own_rows, :]
        other = turned_in[quarter]
        blocks.append(jnp.where(is_first, own, other))
        blocks.append(jnp.where(is_first, other, own))
    even = [blocks[at] + blocks[at + 4] for at in range(4)]
    odd = [blocks[at] - blocks[at + 4] for at in range(4)]

    def beside(parts):
        return jnp.concatenate(parts, axis=1)

    first = rows_by_table(
        beside([even[0] + even[2], even[1] + even[3]]), short_table[0, 0, :256], short_table[0, 1, :256]
    )
    second = rows_by_table(
        beside([even[0] - even[2], even[1] - even[3]]), short_table[0, 0, 256:], short_table[0, 1, 256:]
    )
    third = rows_by_table(beside(odd), long_table[0, 0], long_table[0, 1])
    first = rows_by_table(first * weight_first, short_table[1, 0, :256], short_table[1, 1, :256])
    second = rows_by_table(second * weight_second, short_table[1, 0, 256:], short_table[1, 1, 256:])
    odd = rows_by_table(third * weight_third, long_table[1, 0], long_table[1, 1])
    even = beside([first + second, first - second])
    ahead_half, behind_half = even + odd, even - odd

    def every_other(start):
        return beside(
            [
                values[:, 128 * at : 128 * at + 128]
                for values in (ahead_half, behind_half)
                for at in (start, start + 2)
            ]
        )

    at_even, at_odd = every_other(0), every_other(1)
    back_out[...] = jnp.where(is_first, at_odd, at_even)
    homeward = remote(back_out, back_in, pair_send.at[4], pair_recv.at[4], partner)
    homeward.start()
    fetches[9].wait()
    final[...] = table_by_columns(kx_back[upper, half], jnp.where(is_first, at_even, at_odd))

    def await_sums_ky(step, carry):
        source = (j + 1 + step) % KY_DEVICES
        await_bytes(sums_ky.at[source], sum_recv.at[KX_DEVICES + source])
        return carry

    lax.fori_loop(0, KY_DEVICES - 1, await_sums_ky, 0)
    totals = sums_ky[0]
    for source in range(1, KY_DEVICES):
        totals = totals + sums_ky[source]
    point_total = ROWS * COLUMNS * KX_DEVICES * KY_DEVICES
    means = jnp.sum(totals, axis=1, keepdims=True) * (1.0 / point_total)
    screen = 1.0 / (1.0 + SHIELDING_LEVEL * means[0:1, :])
    field_out[0] = field_x - COUPLING * jnp.sum(means[1:2, :])
    field_out[1] = field_y - COUPLING * jnp.sum(means[2:3, :])

    homeward.wait_recv()
    convolved = final[...] + table_by_columns(kx_back[upper, 1 - half], back_in[...])
    for quarter in range(4):
        leaving[quarter] = convolved[:, 128 * quarter : 128 * quarter + 128]

    def back_target(step):
        quarter = quarter_at(2 * ((step + 1) % 2) + (step // 2) % 2)
        target_i = 2 * ((chip_y + step // 8) % 2) + (half + step // 4) % 2
        return target_i, quarter, 2 * quarter + half

    def send_back(step, carry):
        target_i, quarter, target_j = back_target(step)
        source = leaving.at[quarter, pl.ds(pl.multiple_of(ROWS * target_i, ROWS), ROWS), :]
        own_target = (target_i == i) & (target_j == j)

        @pl.when(jnp.logical_not(own_target))
        def _():
            remote(
                source, conv.at[component], return_send.at[step], return_recv.at[component],
                (target_i, target_j),
            ).start()

        @pl.when(own_target)
        def _():
            pltpu.make_async_copy(source, conv.at[component], return_recv.at[component]).start()

        return carry

    lax.fori_loop(0, COMPONENTS, send_back, 0)

    def await_back(c, carry):
        await_bytes(conv.at[c], return_recv.at[c])
        return carry

    lax.fori_loop(0, COMPONENTS, await_back, 0)

    def rotate(group, carry):
        rows = pl.ds(pl.multiple_of(8 * group, 8), 8)
        coupled = [static_part[c, rows, :] - screen * conv[c, rows, :] for c in range(COMPONENTS)]
        state = [rho[c, rows, :] for c in range(COMPONENTS)]
        rotation = commutator_planes(coupled, state)
        for c in range(COMPONENTS):
            out[c, rows, :] = out[c, rows, :] + rotation[c]
        return carry

    lax.fori_loop(0, ROWS // 8, rotate, 0)

    def drain(step, carry):
        c, target_i, target_j = forward_target(step)

        @pl.when(jnp.logical_not((target_i == i) & (target_j == j)))
        def _():
            await_bytes(rho.at[c], send_sem.at[step])

        back_i, _, back_j = back_target(step)

        @pl.when(jnp.logical_not((back_i == i) & (back_j == j)))
        def _():
            await_bytes(conv.at[component], return_send.at[step])

        return carry

    lax.fori_loop(0, COMPONENTS, drain, 0)

    def drain_weights(step, carry):
        @pl.when(sends_weights & (4 * upper + step != j))
        def _():
            await_bytes(weights_own, weight_send.at[step])

        @pl.when(sends_special)
        def _():
            await_bytes(weight_special, weight_send.at[step])

        return carry

    lax.fori_loop(0, 4, drain_weights, 0)

    def drain_sums(step, carry):
        await_bytes(sums_kx.at[0], sum_send.at[step])
        return carry

    lax.fori_loop(0, KX_DEVICES + KY_DEVICES - 2, drain_sums, 0)
    for copy in halo_copies:
        copy.wait_send()
    homeward.wait_send()
    for quarter in range(4):
        await_bytes(turned_in.at[quarter], pair_send.at[quarter])


def commutator_planes(coupled, state):
    coupled_real, coupled_imaginary = unpack(coupled)
    state_real, state_imaginary = unpack(state)

    def real_part(row, column):
        return product_sum(
            [
                term
                for middle in range(4)
                for term in (
                    (1.0, coupled_real[row][middle], state_real[middle][column]),
                    (-1.0, coupled_imaginary[row][middle], state_imaginary[middle][column]),
                    (-1.0, state_real[row][middle], coupled_real[middle][column]),
                    (1.0, state_imaginary[row][middle], coupled_imaginary[middle][column]),
                )
            ]
        )

    def imaginary_part(row, column):
        if row == column:
            return 2.0 * product_sum(
                [
                    term
                    for middle in range(4)
                    if middle != row
                    for term in (
                        (1.0, coupled_real[row][middle], state_imaginary[middle][column]),
                        (1.0, coupled_imaginary[row][middle], state_real[middle][column]),
                    )
                ]
            )
        return product_sum(
            [
                term
                for middle in range(4)
                for term in (
                    (1.0, coupled_real[row][middle], state_imaginary[middle][column]),
                    (1.0, coupled_imaginary[row][middle], state_real[middle][column]),
                    (-1.0, state_real[row][middle], coupled_imaginary[middle][column]),
                    (-1.0, state_imaginary[row][middle], coupled_real[middle][column]),
                )
            ]
        )

    return (
        [imaginary_part(band, band) for band in range(4)]
        + [imaginary_part(row, column) for row, column in BAND_PAIRS]
        + [-real_part(row, column) for row, column in BAND_PAIRS]
    )


def constant_tables():
    forward, backward = [], []
    for upper in range(2):
        table = kx_table(upper)
        high, low = split_table(table)
        forward.append(np.concatenate([high, high, low], axis=1))
        halves = [split_table(table[rows].T) for rows in (slice(0, 64), slice(64, 128))]
        backward.append(np.stack([np.concatenate([high, high, low], axis=1) for high, low in halves]))
    first, second, third = ky_tables()
    short = [np.concatenate([first, second]), np.concatenate([first.T, second.T])]
    long = [third, third.T]
    return (
        np.stack(forward),
        np.stack(backward),
        np.stack([np.stack(split_table(values)) for values in short]),
        np.stack([np.stack(split_table(values)) for values in long]),
        pick_table().astype(ml_dtypes.bfloat16),
    )


def section_body(packed_state_matrix, energies, dipole_x, dipole_y, interaction, driving_field):
    tables = [jnp.asarray(table) for table in constant_tables()]
    vmem = pl.BlockSpec(memory_space=pltpu.VMEM)
    smem = pl.BlockSpec(memory_space=pltpu.SMEM)
    anywhere = pl.BlockSpec(memory_space=pl.ANY)
    f32 = jnp.float32
    dma = pltpu.SemaphoreType.DMA
    plane_stack = (COMPONENTS, ROWS, COLUMNS)
    return pl.pallas_call(
        section_kernel,
        out_shape=(
            jax.ShapeDtypeStruct(plane_stack, f32),
            jax.ShapeDtypeStruct((2,), f32),
        ),
        in_specs=[anywhere] * 5 + [smem] + [anywhere] * 5,
        out_specs=(vmem, smem),
        scratch_shapes=[
            pltpu.VMEM(plane_stack, f32),
            pltpu.VMEM((4, ROWS, COLUMNS), f32),
            pltpu.VMEM((12, ROWS, COLUMNS), f32),
            pltpu.VMEM((12, ROWS, COLUMNS), f32),
            pltpu.VMEM((16, 1024), f32),
            pltpu.VMEM((2, 128, 384), jnp.bfloat16),
            pltpu.VMEM((2, 2, 128, 192), jnp.bfloat16),
            pltpu.VMEM((4, 128, 128), f32),
            pltpu.VMEM(plane_stack, f32),
            pltpu.VMEM((2, 32, COLUMNS), f32),
            pltpu.VMEM((2, 32, COLUMNS), f32),
            pltpu.VMEM((ROWS, COLUMNS), f32),
            pltpu.VMEM((2, ROWS, COLUMNS), f32),
            pltpu.VMEM((COMPONENTS, 48, COLUMNS), f32),
            pltpu.VMEM((16, 640), f32),
            pltpu.VMEM((32, 640), f32),
            pltpu.VMEM((8, 640), f32),
            pltpu.VMEM((4, 128, 128), f32),
            pltpu.VMEM((4, 64, 128), f32),
            pltpu.VMEM((64, 512), f32),
            pltpu.VMEM((64, 512), f32),
            pltpu.VMEM((128, 512), f32),
            pltpu.VMEM((4, 128, 128), f32),
            pltpu.VMEM((KX_DEVICES, 8, COLUMNS), f32),
            pltpu.VMEM((KY_DEVICES, 8, COLUMNS), f32),
            pltpu.VMEM(plane_stack, f32),
            pltpu.VMEM((2, 2, 512, 256), jnp.bfloat16),
            pltpu.VMEM((2, 2, 512, 512), jnp.bfloat16),
            pltpu.VMEM((1024, 640), jnp.bfloat16),
            dma((10,)),
            dma((16,)),
            dma((16,)),
            dma((4,)),
            dma((4,)),
            dma((4,)),
            dma((3,)),
            dma((5,)),
            dma((5,)),
            dma((16,)),
            dma((16,)),
            dma((10,)),
            dma((12,)),
        ],
        compiler_params=pltpu.CompilerParams(
            collective_id=0, has_side_effects=True, vmem_limit_bytes=64 * 1024 * 1024
        ),
        cost_estimate=pl.CostEstimate(flops=1_200_000_000, bytes_accessed=6_000_000, transcendentals=0),
    )(packed_state_matrix, energies, dipole_x, dipole_y, interaction, driving_field, *tables)


def solution(mesh):
    in_specs = (
        P(None, "kx", "ky"),
        P(None, "kx", "ky"),
        P(None, "kx", "ky"),
        P(None, "kx", "ky"),
        P("ky", None),
        P(),
    )
    out_specs = (P(None, "kx", "ky"), P())
    chosen = section_body if fits_section_kernel(mesh) else body
    return jax.shard_map(chosen, mesh=mesh, in_specs=in_specs, out_specs=out_specs, check_vma=False)
```
